256 devices in a mesh: dp: 32 (over y, z), tp: 8 (over x, core).
Axes of the slice: x: 4, y: 4, z: 8, core: 2. Of those that a mesh axis runs over, the one named last changes fastest.
Arguments:
- queries: bfloat16 [512, 8192], P('dp', 'tp')
- fresh_token_key: bfloat16 [512, 1024], P('dp', 'tp')
- fresh_token_value: bfloat16 [512, 1024], P('dp', 'tp'), may hold values from -6 to 6
- key_value_pool: bfloat16 [20480, 2, 16, 1024], P('dp', None, None, 'tp'), may hold values from -6 to 6
- request_block_map: int32 [512, 32], P('dp'), may hold values from 0 to 639, as said below
- lengths: int32 [512], P('dp'), may hold values from 1 to 512, as said below
- row_counts: int32 [32], replicated, may hold values from 4 to 16, as said below
- move_src: int32 [32, 32, 4], replicated, may hold values from 0 to 639
- move_dst: int32 [32, 32, 4], replicated, may hold values from 0 to 639, as said below
- move_count: int32 [32, 32], replicated, may hold values from 0 to 4, as said below
- residual: bfloat16 [512, 8192], P(None, 'dp'), may hold values from -6 to 6
- out_proj: bfloat16 [8192, 8192], P('tp', 'dp'), may hold values from -1 to 1
- w_gate: bfloat16 [28672, 8192], P(('dp', 'tp')), may hold values from -0.0625 to 0.0625
- w_up: bfloat16 [28672, 8192], P(('dp', 'tp')), may hold values from -0.0625 to 0.0625
- w_down: bfloat16 [28672, 8192], P(('dp', 'tp')), may hold values from -0.15625 to 0.15625
Outputs:
- mixed: bfloat16 [512, 8192], P(None, ('dp', 'tp'))
The draws below stay inside these ranges and needn't reach their ends.
Inputs may be any that keep to these rules, and one draw needn't show every extreme that they name: `request_block_map`: the first 512 blocks named by one rank's slots are distinct blocks of that rank's pool. `lengths`: at least one request has 512 cached tokens. `row_counts`: some rank has all 16 slots live. For a fixed destination rank e, all move_dst[s, e, c] over s and c are distinct. `move_count`: some rank receives 4 blocks from every rank.
All inputs are finite; a program needn't handle non-finite values.
Results may differ from the reference program's by a relative error of at most 0.02.
Values may be sent and summed in bfloat16 or wider, within the bound.
No kernel may reach another device: no remote copies, remote signals or barrier semaphores. Data moves between devices by JAX's collectives and lax.ppermute only.
A program may use at most 128 MiB of HBM per device.

```python
import jax
import jax.numpy as jnp
from jax import lax

D = 8192
QUERY_HEAD_COUNT = 64
KEY_VALUE_HEADS = 8
HEAD_SIZE = 128
FF = 28672
RANK_REQUESTS = 16
BLOCK_TOKENS = 16
REQUEST_BLOCKS = 32
CAP = 4
RANK_POOL_BLOCKS = 640
TOTAL_ROWS = 512
N_DP = 32


def shared_keys(key):
    return jax.random.normal(key, (TOTAL_ROWS, KEY_VALUE_HEADS * HEAD_SIZE), jnp.float32)


def draw_fresh_token_key(key, part):
    base_offset = shared_keys(key)
    return base_offset.astype(jnp.bfloat16)


def draw_queries(key, part):
    key = jax.random.fold_in(key, 12)
    noise = jax.random.normal(key, (TOTAL_ROWS, QUERY_HEAD_COUNT * HEAD_SIZE), jnp.float32)
    result = noise
    return result.astype(jnp.bfloat16)


def draw_row_counts(key, part):
    key = jax.random.fold_in(key, 21)
    count_key, top_key = jax.random.split(key)
    counts = jax.random.randint(count_key, (N_DP,), max(1, RANK_REQUESTS // 4), RANK_REQUESTS + 1)
    fullest = jax.random.randint(top_key, (), 0, N_DP)
    return counts.at[fullest].set(RANK_REQUESTS).astype(jnp.int32)


def draw_lengths(key, part):
    key = jax.random.fold_in(key, 22)
    length_key, top_key = jax.random.split(key)
    longest = REQUEST_BLOCKS * BLOCK_TOKENS
    values = jax.random.randint(length_key, (TOTAL_ROWS,), 1, longest + 1)
    place = jax.random.randint(top_key, (), 0, TOTAL_ROWS)
    return values.at[place].set(longest).astype(jnp.int32)


def draw_request_block_map(key, part):
    key = jax.random.fold_in(key, 23)
    rank_keys = jax.random.split(key, N_DP)
    chosen = jax.vmap(lambda single: jax.random.permutation(single, RANK_POOL_BLOCKS)[:RANK_REQUESTS * REQUEST_BLOCKS])(rank_keys)
    return chosen.reshape(TOTAL_ROWS, REQUEST_BLOCKS).astype(jnp.int32)


def draw_move_dst(key, part):
    key = jax.random.fold_in(key, 24)
    rank_keys = jax.random.split(key, N_DP)
    chosen = jax.vmap(lambda single: jax.random.permutation(single, RANK_POOL_BLOCKS)[:N_DP * CAP])(rank_keys)
    return jnp.transpose(chosen.reshape(N_DP, N_DP, CAP), (1, 0, 2)).astype(jnp.int32)


def draw_move_count(key, part):
    key = jax.random.fold_in(key, 25)
    count_key, full_key = jax.random.split(key)
    counts = jax.random.randint(count_key, (N_DP, N_DP), 0, CAP + 1)
    fullest = jax.random.randint(full_key, (), 0, N_DP)
    return counts.at[:, fullest].set(CAP).astype(jnp.int32)


def set_ends(values, own_key, least, high):
    spot = [jax.random.randint(jax.random.fold_in(own_key, axis), (), 0, length) for axis, length in enumerate(values.shape)]
    widest = values.shape.index(max(values.shape))
    next_to = spot[:widest] + [(spot[widest] + 1) % values.shape[widest]] + spot[widest + 1:]
    return values.at[tuple(spot)].set(least).at[tuple(next_to)].set(high)


def strengthened(values, stream_key, source, target, shards_of, factor):
    owner, partner = [(jnp.arange(values.shape[dim]) // (values.shape[dim] // shards_of)).reshape([-1 if axis == dim else 1 for axis in range(values.ndim)]) for dim in (source, target)]
    chosen = jax.random.permutation(stream_key, shards_of)[partner]
    strong = (owner == chosen) | (owner == (partner + shards_of // 2) % shards_of)
    return jnp.where(strong, factor * values, values)


def block_levels(stream_key, extent, pieces, low, largest):
    level = 1.0
    for axis_at, blocks in pieces:
        steps = jax.random.uniform(jax.random.fold_in(jax.random.fold_in(stream_key, 6), axis_at), (blocks,), jnp.float32, low / len(pieces), largest / len(pieces))
        level = level * jnp.repeat(jnp.exp(steps), extent[axis_at] // blocks).reshape((-1,) + (1,) * (len(extent) - 1 - axis_at))
    return level


def scatter_about(key, extent, scale, reach, cuts=(), kind=jnp.bfloat16):
    gain = block_levels(key, extent, cuts, -0.22, 0.18) if cuts else 1.0
    values = jax.random.normal(key, extent, jnp.float32) * scale * gain
    return jnp.minimum(jnp.maximum(values, -reach), reach).astype(kind)


def gaussian_with(rng, shape, scale, limit, pieces, heavy, kind=jnp.bfloat16):
    drawn = scale * jax.random.normal(rng, shape, jnp.float32)
    if pieces:
        drawn = drawn * block_levels(rng, shape, pieces, -0.22, 0.18)
    return jnp.clip(strengthened(drawn, jax.random.fold_in(rng, 3), *heavy), -limit, limit).astype(kind)


def setup_inputs(seed: int = 0) -> dict:
    key_of = jax.random.split(jax.random.key(seed), 16)
    return {
        "queries": draw_queries(jax.random.fold_in(key_of[15], 71), 0),
        "fresh_token_key": draw_fresh_token_key(jax.random.fold_in(key_of[15], 71), 0),
        "fresh_token_value": scatter_about(key_of[2], (TOTAL_ROWS, KEY_VALUE_HEADS * HEAD_SIZE), 1.0, 6.0, ((0, 32), (1, 8))),
        "key_value_pool": scatter_about(key_of[3], (N_DP * RANK_POOL_BLOCKS, 2, BLOCK_TOKENS, KEY_VALUE_HEADS * HEAD_SIZE), 1.0, 6.0, ((0, 32), (3, 8))),
        "request_block_map": draw_request_block_map(jax.random.fold_in(key_of[15], 71), 0),
        "lengths": draw_lengths(jax.random.fold_in(key_of[15], 71), 0),
        "row_counts": draw_row_counts(jax.random.fold_in(key_of[15], 71), 0),
        "move_src": set_ends(jax.random.randint(key_of[7], (N_DP, N_DP, CAP), 0, RANK_POOL_BLOCKS), jax.random.fold_in(key_of[7], 1), 0, RANK_POOL_BLOCKS - 1).astype(jnp.int32),
        "move_dst": draw_move_dst(jax.random.fold_in(key_of[15], 71), 0),
        "move_count": draw_move_count(jax.random.fold_in(key_of[15], 71), 0),
        "residual": scatter_about(key_of[10], (TOTAL_ROWS, D), 1.0, 6.0, ((1, 32),)),
        "out_proj": scatter_about(key_of[11], (QUERY_HEAD_COUNT * HEAD_SIZE, D), (2 * QUERY_HEAD_COUNT * HEAD_SIZE // (REQUEST_BLOCKS * BLOCK_TOKENS)) ** -0.5, 1.0, ((0, 8), (1, 32))),
        "w_gate": scatter_about(key_of[12], (FF, D), D ** -0.5, 0.0625, ((0, 256),)),
        "w_up": scatter_about(key_of[13], (FF, D), D ** -0.5, 0.0625, ((0, 256),)),
        "w_down": gaussian_with(key_of[14], (FF, D), FF ** -0.5, 0.15625, ((0, 256),), (0, 1, 256, 6.0)),
    }


def attend(queries, fresh_token_key, fresh_token_value, pool_of_blocks, table, lengths):
    slot_count = queries.shape[0]
    kv_heads = fresh_token_key.shape[1] // HEAD_SIZE
    group_size = queries.shape[1] // fresh_token_key.shape[1]
    blocks = pool_of_blocks[table]
    span = table.shape[1] * BLOCK_TOKENS
    keys = blocks[:, :, 0].reshape(slot_count, span, kv_heads, HEAD_SIZE).astype(jnp.float32)
    values = blocks[:, :, 1].reshape(slot_count, span, kv_heads, HEAD_SIZE).astype(jnp.float32)
    query_heads = queries.reshape(slot_count, kv_heads, group_size, HEAD_SIZE).astype(jnp.float32)
    own_keys = fresh_token_key.reshape(slot_count, kv_heads, HEAD_SIZE).astype(jnp.float32)
    own_values = fresh_token_value.reshape(slot_count, kv_heads, 1, HEAD_SIZE).astype(jnp.float32)
    scale = 1.0 / jnp.sqrt(jnp.float32(HEAD_SIZE))
    scores = jnp.einsum('rkgd,rskd->rkgs', query_heads, keys) * scale
    position = jnp.arange(span)
    scores = jnp.where(position[None, None, None, :] < lengths[:, None, None, None], scores, jnp.float32(-1e+30))
    own = jnp.einsum('rkgd,rkd->rkg', query_heads, own_keys) * scale
    top = jnp.maximum(lax.optimization_barrier(jnp.max(scores, axis=-1)), own)
    cached_exp = jnp.exp(scores - top[..., None])
    own_exp = jnp.exp(own - top)
    total = lax.optimization_barrier(jnp.sum(cached_exp, axis=-1)) + own_exp
    cached_w = (cached_exp / total[..., None]).astype(jnp.bfloat16).astype(jnp.float32)
    own_w = (own_exp / total).astype(jnp.bfloat16).astype(jnp.float32)
    result = jnp.einsum('rkgs,rskd->rkgd', cached_w, values) + own_w[..., None] * own_values
    return result.reshape(slot_count, kv_heads * group_size * HEAD_SIZE).astype(jnp.bfloat16)

def reference(queries, fresh_token_key, fresh_token_value, key_value_pool, request_block_map, lengths, row_counts, move_src, move_dst, move_count, residual, out_proj, w_gate, w_up, w_down):
    source_rank = jnp.arange(N_DP, dtype=jnp.int32)[:, None, None]
    target_rank = jnp.arange(N_DP, dtype=jnp.int32)[None, :, None]
    slot_range = jnp.arange(CAP, dtype=jnp.int32)[None, None, :]
    usable = slot_range < move_count[:, :, None]
    source_rows = (source_rank * RANK_POOL_BLOCKS + move_src).reshape(-1)
    target_rows = jnp.where(usable, target_rank * RANK_POOL_BLOCKS + move_dst, N_DP * RANK_POOL_BLOCKS).reshape(-1)
    pool_of_blocks = key_value_pool.at[target_rows].set(key_value_pool[source_rows], mode='drop')
    pool_by_rank = pool_of_blocks.reshape(N_DP, RANK_POOL_BLOCKS, 2, BLOCK_TOKENS, KEY_VALUE_HEADS * HEAD_SIZE)

    def rank_slices(items):
        return attend(items[0], items[1], items[2], items[3], items[4], items[5])
    attended_rows = lax.map(rank_slices, (queries.reshape(N_DP, RANK_REQUESTS, QUERY_HEAD_COUNT * HEAD_SIZE), fresh_token_key.reshape(N_DP, RANK_REQUESTS, KEY_VALUE_HEADS * HEAD_SIZE), fresh_token_value.reshape(N_DP, RANK_REQUESTS, KEY_VALUE_HEADS * HEAD_SIZE), pool_by_rank, request_block_map.reshape(N_DP, RANK_REQUESTS, REQUEST_BLOCKS), lengths.reshape(N_DP, RANK_REQUESTS)))
    attended_rows = attended_rows.reshape(TOTAL_ROWS, QUERY_HEAD_COUNT * HEAD_SIZE)
    projected = jnp.dot(attended_rows, out_proj, preferred_element_type=jnp.float32)
    row_index = jnp.arange(TOTAL_ROWS, dtype=jnp.int32)
    active = row_index % RANK_REQUESTS < row_counts[row_index // RANK_REQUESTS]
    stream = jnp.where(active[:, None], residual.astype(jnp.float32) + projected, jnp.float32(0.0)).astype(jnp.bfloat16)
    dims = (((1,), (1,)), ((), ()))
    gate_sum = lax.dot_general(stream, w_gate, dims, preferred_element_type=jnp.float32)
    up_sum = lax.dot_general(stream, w_up, dims, preferred_element_type=jnp.float32)
    hidden = (jax.nn.silu(gate_sum) * up_sum).astype(jnp.bfloat16)
    down_sum = jnp.dot(hidden, w_down, preferred_element_type=jnp.float32)
    return (stream.astype(jnp.float32) + down_sum).astype(jnp.bfloat16)
```

```python
import jax
import jax.numpy as jnp
import numpy as np
from jax import lax
from jax.experimental import pallas as pl
from jax.experimental.pallas import tpu as pltpu
from jax.sharding import Mesh, PartitionSpec as P

HEAD = 128
GROUP = 8
TOKENS = 16
BF = jnp.bfloat16
F32 = jnp.float32
NT = (((1,), (1,)), ((), ()))
NN = (((1,), (0,)), ((), ()))
REL = (0, 3, 1, 2)


def params(mib):
    return pltpu.CompilerParams(vmem_limit_bytes=mib * 2**20)


def vmem(n):
    return [pl.BlockSpec(memory_space=pltpu.VMEM)] * n


SMEM = pl.BlockSpec(memory_space=pltpu.SMEM)
ANY = pl.BlockSpec(memory_space=pl.ANY)


def weights_kernel(order_ref, gate_ref, up_ref, down_ref, own_ref, other_ref, down_own, down_other):
    order = order_ref[...]
    for j in range(gate_ref.shape[1] // 256):
        cols = slice(256 * j, 256 * j + 256)
        half = slice(128 * j, 128 * j + 128)
        for n, ref in enumerate((gate_ref, up_ref)):
            moved = lax.dot_general(ref[:, cols], order, NT, preferred_element_type=F32).astype(BF)
            own_ref[n, :, half] = moved[:, :128]
            other_ref[n, :, half] = moved[:, 128:]
        moved = lax.dot_general(order, down_ref[:, cols], NT, preferred_element_type=F32).astype(BF)
        down_own[half, :] = moved[:128]
        down_other[half, :] = moved[128:]


def split_weights(order, w_gate, w_up, w_down):
    rows, width = w_gate.shape
    step = 1024
    half = step // 2
    return pl.pallas_call(
        weights_kernel,
        grid=(width // step,),
        in_specs=[pl.BlockSpec((256, 256), lambda i: (0, 0))]
        + [pl.BlockSpec((rows, step), lambda i: (0, i))] * 3,
        out_specs=[pl.BlockSpec((2, rows, half), lambda i: (0, 0, i))] * 2
        + [pl.BlockSpec((half, rows), lambda i: (i, 0))] * 2,
        out_shape=[jax.ShapeDtypeStruct((2, rows, width // 2), BF)] * 2
        + [jax.ShapeDtypeStruct((width // 2, rows), BF)] * 2,
        compiler_params=params(32),
    )(order, w_gate, w_up, w_down)


def attention_kernel(
    table, lengths, q_ref, key_ref, value_ref, pool_ref, arrived_ref, out_ref,
    blocks, keys, values, scores, weights, result, sems,
):
    slots, depth = table.shape
    pool_size = pool_ref.shape[0]
    span = depth * TOKENS
    first = pltpu.make_async_copy(pool_ref, blocks.at[pl.ds(0, pool_size)], sems.at[0])
    second = pltpu.make_async_copy(
        arrived_ref, blocks.at[pl.ds(pool_size, arrived_ref.shape[0])], sems.at[1]
    )
    first.start()
    second.start()
    first.wait()
    second.wait()

    def fetch(i, carry):
        for j in range(depth):
            block = table[i, j]
            keys[i, j * TOKENS : (j + 1) * TOKENS, :] = blocks[block, 0]
            values[i, j * TOKENS : (j + 1) * TOKENS, :] = blocks[block, 1]
        return carry

    lax.fori_loop(0, slots, fetch, 0)
    scale = np.float32(1.0) / np.sqrt(np.float32(HEAD))
    position = lax.broadcasted_iota(jnp.int32, (GROUP, span), 1)
    for i in range(slots):
        q = q_ref[i * GROUP : (i + 1) * GROUP, :]
        s = lax.dot_general(q.astype(BF), keys[i], NT, preferred_element_type=F32) * scale
        scores[i * GROUP : (i + 1) * GROUP, :] = jnp.where(position < lengths[i], s, F32(-1e30))
        own = jnp.sum(q * key_ref[i : i + 1, :], axis=1, keepdims=True) * scale
        result[i * GROUP : (i + 1) * GROUP, :] = jnp.broadcast_to(own, (GROUP, HEAD))
    s = scores[...]
    own = result[:, :1]
    top = jnp.maximum(jnp.max(s, axis=1, keepdims=True), own)
    e = jnp.exp(s - top)
    own_e = jnp.exp(own - top)
    total = jnp.sum(e, axis=1, keepdims=True) + own_e
    weights[...] = e / total
    own_w = (own_e / total).astype(BF).astype(F32)
    result[...] = jnp.broadcast_to(own_w, result.shape)
    for i in range(slots):
        rows = slice(i * GROUP, (i + 1) * GROUP)
        o = lax.dot_general(weights[rows, :].astype(BF), values[i], NN, preferred_element_type=F32)
        result[rows, :] = o + result[rows, :] * value_ref[i : i + 1, :]
    for h in range(GROUP):
        out_ref[:, h * HEAD : (h + 1) * HEAD] = result[pl.ds(h, slots, stride=GROUP), :].astype(BF)


def attention(table, lengths, queries, fresh_key, fresh_value, pool, arrived):
    slots, depth = table.shape
    span = depth * TOKENS
    total = pool.shape[0] + arrived.shape[0]
    return pl.pallas_call(
        attention_kernel,
        in_specs=[SMEM, SMEM] + vmem(3) + [ANY, ANY],
        out_specs=pl.BlockSpec(memory_space=pltpu.VMEM),
        out_shape=jax.ShapeDtypeStruct(queries.shape, BF),
        scratch_shapes=[
            pltpu.VMEM((total,) + pool.shape[1:], BF),
            pltpu.VMEM((slots, span, HEAD), BF),
            pltpu.VMEM((slots, span, HEAD), BF),
            pltpu.VMEM((slots * GROUP, span), F32),
            pltpu.VMEM((slots * GROUP, span), F32),
            pltpu.VMEM((slots * GROUP, HEAD), F32),
            pltpu.SemaphoreType.DMA((2,)),
        ],
        compiler_params=params(40),
    )(
        table,
        lengths,
        queries.reshape(slots * GROUP, HEAD).astype(F32),
        fresh_key.astype(F32),
        fresh_value.astype(F32),
        pool,
        arrived,
    )


def project_kernel(coords, place_ref, weight_ref, a0, a1, l0, l1, r0, r1, o0, o1, out_ref):
    width = out_ref.shape[1]
    lane = lax.broadcasted_iota(jnp.int32, (width, place_ref.shape[2]), 0)
    half = a0.shape[0]
    packed = jnp.zeros((width, a0.shape[1]), F32)
    for off, pair in zip(REL, ((a0, a1), (l0, l1), (r0, r1), (o0, o1))):
        y = lax.rem(coords[0] + off, 4)
        pick = (lane == place_ref[y]).astype(BF)
        for n, ref in enumerate(pair):
            packed += lax.dot_general(
                pick[:, n * half : (n + 1) * half], ref[...], NN, preferred_element_type=F32
            )
    out_ref[...] = lax.dot_general(
        weight_ref[...], packed.astype(BF), NT, preferred_element_type=F32
    ).astype(BF)


def project(coords, place, weight, pieces, width):
    return pl.pallas_call(
        project_kernel,
        in_specs=[SMEM] + vmem(10),
        out_specs=pl.BlockSpec(memory_space=pltpu.VMEM),
        out_shape=jax.ShapeDtypeStruct((weight.shape[0], width), BF),
        compiler_params=params(32),
    )(coords, place, weight, *pieces)


def assemble(coords, pieces, part, stream):
    inner, outer = (0, 1) if part == 0 else (1, 0)
    for r3, pair in enumerate(pieces):
        far = lax.rem(coords[outer] + REL[r3], 4)
        for h in range(2):
            for k in range(2):
                near = lax.rem(coords[inner] + REL[2 * h + k], 4)
                y, x = (near, far) if part == 0 else (far, near)
                for z in range(8):
                    row = (y * 8 + z) * 128 + part * 64 + x * 16
                    stream[pl.ds(pl.multiple_of(row, 16), 16), :] = pair[h][k * 8 + z]


def up_kernel(coords, own_ref, other_ref, *refs):
    pieces, out_own, out_other, stream = refs[:16], refs[16], refs[17], refs[18]
    for part in range(2):
        mine = pieces[8 * part : 8 * part + 8]
        assemble(coords, [mine[2 * k : 2 * k + 2] for k in range(4)], part, stream)
    s = stream[...]
    for n in range(2):
        out_own[n] = lax.dot_general(own_ref[n], s, NN, preferred_element_type=F32)
        out_other[n] = lax.dot_general(other_ref[n], s, NN, preferred_element_type=F32)


def gate_up(coords, own, other, pieces):
    width = pieces[0].shape[-1]
    return pl.pallas_call(
        up_kernel,
        in_specs=[SMEM] + vmem(18),
        out_specs=vmem(2),
        out_shape=[jax.ShapeDtypeStruct((2, own.shape[1], width), F32)] * 2,
        scratch_shapes=[pltpu.VMEM((own.shape[2], width), BF)],
        compiler_params=params(48),
    )(coords, own, other, *pieces)


def down_kernel(coords, down_own, down_other, gu_own, gu_other, in_own, in_other, *refs):
    outs, partial = refs[:16], refs[16]
    hidden = []
    for mine, theirs in ((gu_own, in_own), (gu_other, in_other)):
        gate = mine[0] + theirs[0]
        up = mine[1] + theirs[1]
        hidden.append((gate * jax.nn.sigmoid(gate) * up).astype(BF))
    step = 512
    for n in range(partial.shape[0] // step):
        rows = slice(n * step, (n + 1) * step)
        partial[rows, :] = (
            lax.dot_general(down_own[rows, :], hidden[0], NN, preferred_element_type=F32)
            + lax.dot_general(down_other[rows, :], hidden[1], NN, preferred_element_type=F32)
        ).astype(BF)
    for part in range(2):
        inner, outer = (0, 1) if part == 0 else (1, 0)
        for r3 in range(4):
            far = lax.rem(coords[outer] + REL[r3], 4)
            for h in range(2):
                out = outs[8 * part + 2 * r3 + h]
                for k in range(2):
                    near = lax.rem(coords[inner] + REL[2 * h + k], 4)
                    y, x = (near, far) if part == 0 else (far, near)
                    for z in range(8):
                        row = (y * 8 + z) * 128 + part * 64 + x * 16
                        out[k * 8 + z] = partial[pl.ds(pl.multiple_of(row, 16), 16), :]


def down(coords, down_own, down_other, gu_own, gu_other, in_own, in_other):
    width = gu_own.shape[2]
    return pl.pallas_call(
        down_kernel,
        in_specs=[SMEM] + vmem(6),
        out_specs=vmem(16),
        out_shape=[jax.ShapeDtypeStruct((16, 16, width), BF)] * 16,
        scratch_shapes=[pltpu.VMEM((down_own.shape[0], width), BF)],
        compiler_params=params(48),
    )(coords, down_own, down_other, gu_own, gu_other, in_own, in_other)


def finish_kernel(place_ref, stream_ref, sums_ref, out_ref):
    total = stream_ref[...].astype(F32) + jnp.sum(sums_ref[...].astype(F32), axis=0)
    width = total.shape[1]
    mixed = total.astype(BF)
    per = place_ref.shape[2]
    lane = lax.broadcasted_iota(jnp.int32, (width, per), 0)
    for y in range(place_ref.shape[0]):
        pick = (lane == place_ref[y]).astype(BF)
        out_ref[:, y * per : (y + 1) * per] = lax.dot_general(
            mixed, pick, NN, preferred_element_type=F32
        ).astype(BF)


def finish(place, stream, sums):
    return pl.pallas_call(
        finish_kernel,
        in_specs=vmem(3),
        out_specs=pl.BlockSpec(memory_space=pltpu.VMEM),
        out_shape=jax.ShapeDtypeStruct((stream.shape[0], place.shape[0] * place.shape[2]), BF),
        compiler_params=params(16),
    )(place, stream, sums)


def shift(a, axis, by):
    return lax.ppermute(a, axis, [(i, (i + by) % 4) for i in range(4)])


def ring_gather(a0, a1, axis):
    l0, r1 = shift(a0, axis, 1), shift(a1, axis, -1)
    l1, r0 = shift(a1, axis, 1), shift(a0, axis, -1)
    return a0, a1, l0, l1, r0, r1, shift(l0, axis, 1), shift(r1, axis, -1)


def add(*terms):
    return sum(t.astype(F32) for t in terms).astype(BF)


def ring_scatter(own0, own1, l0, l1, r0, r1, o0, o1, axis):
    from_left, from_right = shift(o0, axis, 1), shift(o1, axis, -1)
    c1, d0 = shift(r1, axis, 1), shift(l0, axis, -1)
    c0 = shift(add(r0, from_left), axis, 1)
    d1 = shift(add(l1, from_right), axis, -1)
    return add(own0, c0, d0), add(own1, c1, d1)


def all_to_all(a, axis):
    return lax.all_to_all(a, axis, split_axis=0, concat_axis=0, tiled=True)


def mlp(width, coords, place, out_weight, rows, residual, weights, down_weights):
    partial = project(coords, place, out_weight, rows, width)
    arrived = all_to_all(partial.reshape(8, 32, width), ("x", "core"))
    piece = (residual[:, :width].astype(F32) + jnp.sum(arrived.astype(F32), axis=0)).astype(BF)
    spread = all_to_all(jnp.broadcast_to(piece[None], (8, 32, width)), "z")
    pieces = []
    for part, (near, far) in enumerate((("y", "x"), ("x", "y"))):
        mine = spread[:, 16 * part : 16 * part + 16]
        a0, a1, l0, l1, r0, r1, o0, o1 = ring_gather(mine[:4], mine[4:], near)
        pieces += ring_gather(
            jnp.concatenate([a0, a1, l0, l1]), jnp.concatenate([r0, r1, o0, o1]), far
        )
    gu_own, gu_other = gate_up(coords, *weights, pieces)
    swap = [(0, 1), (1, 0)]
    in_other = lax.ppermute(gu_own, "core", swap)
    in_own = lax.ppermute(gu_other, "core", swap)
    partials = down(coords, *down_weights, gu_own, gu_other, in_own, in_other)
    halves = []
    for part, (near, far) in enumerate((("y", "x"), ("x", "y"))):
        s0, s1 = ring_scatter(*partials[8 * part : 8 * part + 8], far)
        halves.append(
            jnp.concatenate(
                ring_scatter(
                    s0[:4], s0[4:8], s0[8:12], s0[12:], s1[:4], s1[4:8], s1[8:12], s1[12:], near
                )
            )
        )
    sums = all_to_all(jnp.concatenate(halves, axis=1), "z")
    return finish(place, piece, sums)


def per_device(
    queries,
    fresh_token_key,
    fresh_token_value,
    key_value_pool,
    request_block_map,
    lengths,
    row_counts,
    move_src,
    move_dst,
    move_count,
    residual,
    out_proj,
    w_gate,
    w_up,
    w_down,
):
    x, y, core = lax.axis_index("x"), lax.axis_index("y"), lax.axis_index("core")
    rank = lax.axis_index(("y", "z"))
    group = lax.axis_index(("x", "core"))
    coords = jnp.stack([y, x]).astype(jnp.int32)
    ranks, _, cap = move_src.shape
    slots = queries.shape[0]
    pool_size = key_value_pool.shape[0]

    source = lax.dynamic_index_in_dim(move_src, rank, 0, keepdims=False).reshape(-1)
    parcel = key_value_pool[source].reshape((ranks, cap) + key_value_pool.shape[1:])
    arrived = all_to_all(parcel, ("y", "z")).reshape((ranks * cap,) + key_value_pool.shape[1:])
    target = lax.dynamic_index_in_dim(move_dst, rank, 1, keepdims=False)
    count = lax.dynamic_index_in_dim(move_count, rank, 1, keepdims=False)
    target = jnp.where(jnp.arange(cap)[None, :] < count[:, None], target, -1).reshape(-1)
    hit = request_block_map[:, :, None] == target[None, None, :]
    number = pool_size + jnp.arange(ranks * cap, dtype=jnp.int32)
    table = jnp.max(jnp.where(hit, number, request_block_map[:, :, None]), axis=2)

    row = jnp.arange(ranks * slots, dtype=jnp.int32)
    counts = row_counts[:, None]
    before = jnp.sum(
        jnp.where(jnp.arange(ranks)[None, :] < jnp.arange(ranks)[:, None], row_counts[None, :], 0),
        axis=1,
    )
    slot = jnp.arange(slots, dtype=jnp.int32)[None, :]
    place = jnp.where(slot < counts, before[:, None] + slot, -1).astype(jnp.int32)
    live = jnp.sum(row_counts)
    place = place.reshape(4, 1, ranks * slots // 4)

    n = np.arange(256)
    which, part, xs, j = n // 128, n // 64 % 2, n // 16 % 4, n % 16
    column = 64 * xs + 16 * part + j
    owner = jnp.where(which == 0, core, 1 - core)
    order = (jnp.arange(256)[None, :] == (column + 32 * owner)[:, None]).astype(BF)
    up_own, up_other, down_own, down_other = split_weights(order, w_gate, w_up, w_down)
    swap = [(0, 1), (1, 0)]
    weights = (up_own, lax.ppermute(up_other, "core", swap))
    down_weights = (down_own, lax.ppermute(down_other, "core", swap))
    out_weight = out_proj.T
    mine = lax.dynamic_slice_in_dim(residual, group * 32, 32, 1)
    pick = (place.reshape(-1)[:, None] == row[None, :]).astype(BF)
    mine = lax.dot_general(
        mine, pick, (((0,), (0,)), ((), ())), preferred_element_type=F32
    ).astype(BF)

    attended = attention(
        table, lengths, queries, fresh_token_key, fresh_token_value, key_value_pool, arrived
    )
    spread = all_to_all(jnp.broadcast_to(attended[None], (8,) + attended.shape), "z")
    spread = spread.reshape(8 * slots, attended.shape[1])
    rows = ring_gather(spread[: 4 * slots], spread[4 * slots :], "y")
    widths = (256, 384, 512)
    branch = (live > 256).astype(jnp.int32) + (live > 384).astype(jnp.int32)

    def of(width):
        return lambda *args: mlp(width, *args)

    out = lax.switch(
        branch,
        [of(w) for w in widths],
        coords, place, out_weight, rows, mine, weights, down_weights,
    )
    return out.T


def solution(mesh):
    mesh = Mesh(mesh.devices.reshape(4, 8, 4, 2), ("y", "z", "x", "core"))
    dp, tp = ("y", "z"), ("x", "core")
    return jax.shard_map(
        per_device,
        mesh=mesh,
        in_specs=(
            P(dp, tp),
            P(dp, tp),
            P(dp, tp),
            P(dp, None, None, tp),
            P(dp, None),
            P(dp),
            P(),
            P(),
            P(),
            P(),
            P(None, dp),
            P(tp, dp),
            P(dp + tp, None),
            P(dp + tp, None),
            P(dp + tp, None),
        ),
        out_specs=P(None, dp + tp),
        check_vma=False,
    )
```

```python
import jax
import jax.numpy as jnp
import numpy as np
from jax import lax
from jax.experimental import pallas as pl
from jax.experimental.pallas import tpu as pltpu
from jax.sharding import Mesh, PartitionSpec as P

HEAD = 128
GROUP = 8
TOKENS = 16
BF = jnp.bfloat16
F32 = jnp.float32
SCALE = np.float32(1.0) / np.sqrt(np.float32(HEAD))
NT = (((1,), (1,)), ((), ()))
NN = (((1,), (0,)), ((), ()))
REL = (0, 3, 1, 2)


def params(mib):
    return pltpu.CompilerParams(vmem_limit_bytes=mib * 2**20)


def vmem(n):
    return [pl.BlockSpec(memory_space=pltpu.VMEM)] * n


SMEM = pl.BlockSpec(memory_space=pltpu.SMEM)
ANY = pl.BlockSpec(memory_space=pl.ANY)


def weights_kernel(order_ref, gate_ref, up_ref, down_ref, own_ref, other_ref, down_own, down_other):
    order = order_ref[...]
    for j in range(gate_ref.shape[1] // 256):
        cols = slice(256 * j, 256 * j + 256)
        half = slice(128 * j, 128 * j + 128)
        for n, ref in enumerate((gate_ref, up_ref)):
            moved = lax.dot_general(ref[:, cols], order, NT, preferred_element_type=F32).astype(BF)
            rows = slice(n * moved.shape[0], (n + 1) * moved.shape[0])
            own_ref[rows, half] = moved[:, :128]
            other_ref[rows, half] = moved[:, 128:]
        moved = lax.dot_general(order, down_ref[:, cols], NT, preferred_element_type=F32).astype(BF)
        rows = moved.shape[1]
        for ref, part in ((down_own, moved[:128]), (down_other, moved[128:])):
            ref[half, :rows] = part
            ref[half, rows:] = jnp.zeros((128, ref.shape[1] - rows), BF)


def split_weights(order, w_gate, w_up, w_down):
    rows, width = w_gate.shape
    step = 1024
    half = step // 2
    return pl.pallas_call(
        weights_kernel,
        grid=(width // step,),
        in_specs=[pl.BlockSpec((256, 256), lambda i: (0, 0))]
        + [pl.BlockSpec((rows, step), lambda i: (0, i))] * 3,
        out_specs=[pl.BlockSpec((2 * rows, half), lambda i: (0, i))] * 2
        + [pl.BlockSpec((half, HEAD), lambda i: (i, 0))] * 2,
        out_shape=[jax.ShapeDtypeStruct((2 * rows, width // 2), BF)] * 2
        + [jax.ShapeDtypeStruct((width // 2, HEAD), BF)] * 2,
        compiler_params=params(58),
    )(order, w_gate, w_up, w_down)


def load_pool(pool_ref, blocks, sems):
    parts = sems.shape[0]
    rows = blocks.shape[0] // parts
    loads = [
        pltpu.make_async_copy(
            pool_ref.at[pl.ds(n * rows, rows)], blocks.at[pl.ds(n * rows, rows)], sems.at[n]
        )
        for n in range(parts)
    ]
    for load in loads:
        load.start()
    for load in loads:
        load.wait()


def parcel_kernel(source, pool_ref, out_ref, blocks, sems):
    load_pool(pool_ref, blocks, sems)

    def pick(n, carry):
        out_ref[n] = blocks[source[n]]
        return carry

    lax.fori_loop(0, out_ref.shape[0], pick, 0, unroll=8)


def parcels(source, pool):
    return pl.pallas_call(
        parcel_kernel,
        in_specs=[SMEM, ANY],
        out_specs=pl.BlockSpec(memory_space=pltpu.VMEM),
        out_shape=jax.ShapeDtypeStruct(source.shape + pool.shape[1:], BF),
        scratch_shapes=[pltpu.VMEM(pool.shape, BF), pltpu.SemaphoreType.DMA((8,))],
        compiler_params=params(58),
    )(source, pool)


def pool_kernel(
    table, q_ref, key_ref, value_ref, allowed_ref, pool_ref,
    out_ref, top_ref, total_ref, keys, values, scores,
):
    slots, depth = table.shape

    def fetch(i, carry):
        for j in range(depth):
            block = table[i, j]
            keys[i, j * TOKENS : (j + 1) * TOKENS, :] = pool_ref[block, 0]
            values[i, j * TOKENS : (j + 1) * TOKENS, :] = pool_ref[block, 1]
        return carry

    lax.fori_loop(0, slots, fetch, 0)
    for i in range(slots):
        rows = slice(i * GROUP, (i + 1) * GROUP)
        q = q_ref[rows, :]
        s = lax.dot_general(q.astype(BF), keys[i], NT, preferred_element_type=F32) * SCALE
        scores[rows, :] = jnp.where(allowed_ref[i : i + 1, :] > 0, s, F32(-1e30))
        own = jnp.sum(q * key_ref[i : i + 1, :], axis=1, keepdims=True) * SCALE
        out_ref[rows, :] = jnp.broadcast_to(own, (GROUP, HEAD))
    s = scores[...]
    own = out_ref[:, :1]
    top = jnp.maximum(jnp.max(s, axis=1, keepdims=True), own)
    e = jnp.where(s > F32(-1e29), jnp.exp(s - top), F32(0.0))
    own_e = jnp.exp(own - top)
    total = jnp.sum(e, axis=1, keepdims=True) + own_e
    scores[...] = e
    top_ref[...] = jnp.broadcast_to(top, top_ref.shape)
    total_ref[...] = jnp.broadcast_to(total, total_ref.shape)
    out_ref[...] = jnp.broadcast_to(own_e.astype(BF).astype(F32), out_ref.shape)
    for i in range(slots):
        rows = slice(i * GROUP, (i + 1) * GROUP)
        o = lax.dot_general(scores[rows, :].astype(BF), values[i], NN, preferred_element_type=F32)
        out_ref[rows, :] = o + out_ref[rows, :] * value_ref[i : i + 1, :]


def attend_pool(table, queries, fresh_key, fresh_value, allowed, pool):
    slots, depth = table.shape
    span = depth * TOKENS
    return pl.pallas_call(
        pool_kernel,
        in_specs=[SMEM] + vmem(5),
        out_specs=vmem(3),
        out_shape=[jax.ShapeDtypeStruct(queries.shape, F32)] * 3,
        scratch_shapes=[
            pltpu.VMEM((slots, span, HEAD), BF),
            pltpu.VMEM((slots, span, HEAD), BF),
            pltpu.VMEM((slots * GROUP, span), F32),
        ],
        compiler_params=params(20),
    )(table, queries, fresh_key, fresh_value, allowed, pool)


def moved_kernel(q_ref, owner_ref, arrived_ref, part_ref, top_ref, total_ref, out_ref, result):
    blocks = arrived_ref.shape[0]
    keys = arrived_ref[:, 0].reshape(blocks * TOKENS, HEAD)
    values = arrived_ref[:, 1].reshape(blocks * TOKENS, HEAD)
    s = lax.dot_general(q_ref[...].astype(BF), keys, NT, preferred_element_type=F32) * SCALE
    slot = lax.broadcasted_iota(jnp.int32, s.shape, 0) >> 3
    mine = slot == owner_ref[...]
    before = top_ref[:, :1]
    top = jnp.maximum(before, jnp.max(jnp.where(mine, s, F32(-1e30)), axis=1, keepdims=True))
    e = jnp.where(mine, jnp.exp(s - top), F32(0.0))
    keep = jnp.exp(before - top)
    total = total_ref[:, :1] * keep + jnp.sum(e, axis=1, keepdims=True)
    o = lax.dot_general(e.astype(BF), values, NN, preferred_element_type=F32)
    result[...] = (part_ref[...] * keep + o) / total
    slots = out_ref.shape[1]
    for h in range(GROUP):
        head = result[pl.ds(h, slots, stride=GROUP), :].astype(BF)
        for n in range(out_ref.shape[0]):
            out_ref[n, :, h * HEAD : (h + 1) * HEAD] = head


def attend_moved(queries, owner, arrived, part, top, total):
    slots = queries.shape[0] // GROUP
    return pl.pallas_call(
        moved_kernel,
        in_specs=vmem(6),
        out_specs=pl.BlockSpec(memory_space=pltpu.VMEM),
        out_shape=jax.ShapeDtypeStruct((8, slots, GROUP * HEAD), BF),
        scratch_shapes=[pltpu.VMEM(queries.shape, F32)],
        compiler_params=params(24),
    )(queries, owner, arrived, part, top, total)


def project_kernel(coords, rows_ref, own, left, right, opposite, out_ref, mine_ref):
    rows = rows_ref[...]
    y = coords[0]
    for off, ref in zip(REL, (own, left, right, opposite)):
        base = pl.multiple_of(lax.rem(y + off, 4) * 32, 32)
        for part in range(2):
            at = 144 * part
            cols = lax.dot_general(
                ref[at : at + 128, :], rows, NT, preferred_element_type=F32
            ).astype(BF)
            for n in range(4):
                out_ref[4 * part + n, pl.ds(base, 32), :] = cols[32 * n : 32 * n + 32]
            mine_ref[pl.ds(pl.multiple_of(base + 16 * part, 16), 16), :] = ref[
                at + 128 : at + 144, pl.ds(pl.multiple_of(y * 128, 128), 128)
            ]


def project(coords, rows, pieces):
    count = rows.shape[0]
    return pl.pallas_call(
        project_kernel,
        in_specs=[SMEM] + vmem(5),
        out_specs=vmem(2),
        out_shape=[
            jax.ShapeDtypeStruct((8, 128, count), BF),
            jax.ShapeDtypeStruct((128, count), BF),
        ],
        compiler_params=params(32),
    )(coords, rows, *pieces)


def up_kernel(coords, own_hbm, other_hbm, *refs):
    pieces, out_own, out_other, out_mine, stream, weights, sems = refs[:10], *refs[10:]
    rows = own_hbm.shape[0]
    loads = [
        pltpu.make_async_copy(own_hbm, weights.at[pl.ds(0, rows)], sems.at[0]),
        pltpu.make_async_copy(other_hbm, weights.at[pl.ds(rows, rows)], sems.at[1]),
    ]
    for load in loads:
        load.start()
    for part in range(2):
        own, left, right, far0, far1 = pieces[5 * part : 5 * part + 5]
        inner, outer = (0, 1) if part == 0 else (1, 0)
        for r3 in range(4):
            far = lax.rem(coords[outer] + REL[r3], 4)
            for r2 in range(4):
                near = lax.rem(coords[inner] + REL[r2], 4)
                y, x = (near, far) if part == 0 else (far, near)
                start = x * 16
                lane = pl.ds(pl.multiple_of(y * 128, 128), 128)
                for n in range(32):
                    if r3 < 3:
                        chunk = (own, left, right)[r3][r2 * 32 + n]
                    else:
                        chunk = (far0, far1)[r2 // 2][r2 % 2 * 32 + n]
                    row = (n % 4 * 8 + n // 4) * 128 + part * 64
                    stream[pl.ds(pl.multiple_of(row + start, 16), 16), lane] = chunk
    for load, out, at in zip(loads, (out_own, out_other), (0, rows)):
        load.wait()
        out[...] = lax.dot_general(
            weights[at : at + rows, :], stream[...], NN, preferred_element_type=F32
        ).reshape(out.shape)
    for part in range(2):
        row = (coords[0] * 8 + coords[2]) * 128 + part * 64 + coords[1] * 16
        out_mine[16 * part : 16 * part + 16, :] = stream[pl.ds(pl.multiple_of(row, 16), 16), :]


def gate_up(coords, own, other, pieces):
    width = 512
    return pl.pallas_call(
        up_kernel,
        in_specs=[SMEM, ANY, ANY] + vmem(10),
        out_specs=vmem(3),
        out_shape=[jax.ShapeDtypeStruct((2, own.shape[0] // 2, width), F32)] * 2
        + [jax.ShapeDtypeStruct((32, width), BF)],
        scratch_shapes=[
            pltpu.VMEM((own.shape[1], width), BF),
            pltpu.VMEM((2 * own.shape[0], own.shape[1]), BF),
            pltpu.SemaphoreType.DMA((2,)),
        ],
        compiler_params=params(48),
    )(coords, own, other, *pieces)


def chunk_of(coords, part, r3, nears, weight_refs, hidden, gathered):
    inner, outer = (0, 1) if part == 0 else (1, 0)
    far = lax.rem(coords[outer] + REL[r3], 4)
    total = None
    for ref, h in zip(weight_refs, hidden):
        for k, r2 in enumerate(nears):
            near = lax.rem(coords[inner] + REL[r2], 4)
            y, x = (near, far) if part == 0 else (far, near)
            for z in range(8):
                row = (y * 8 + z) * 128 + part * 64 + x * 16
                at = (k * 8 + z) * 16
                gathered[at : at + 16, :] = ref[pl.ds(pl.multiple_of(row, 16), 16), :]
        lhs = gathered[: len(nears) * 128, :]
        term = lax.dot_general(lhs, h, NN, preferred_element_type=F32)
        total = term if total is None else total + term
    return total.reshape(len(nears) * 8, 16, total.shape[1])


def far_kernel(coords, down_own, down_other, gu_own, gu_other, in_own, in_other, *refs):
    outs, hidden_ref, gathered = refs[:4], refs[4], refs[5]
    for n, (mine, theirs) in enumerate(((gu_own, in_own), (gu_other, in_other))):
        gate = mine[0] + theirs[0]
        up = mine[1] + theirs[1]
        rows = gate.shape[0]
        hidden_ref[n, :rows, :] = (gate * jax.nn.sigmoid(gate) * up).astype(BF)
        hidden_ref[n, rows:, :] = jnp.zeros((hidden_ref.shape[1] - rows, gate.shape[1]), BF)
    hidden = [hidden_ref[n] for n in range(2)]
    weights = (down_own, down_other)
    for part in range(2):
        for half in range(2):
            nears = (2 * half, 2 * half + 1)
            outs[2 * part + half][...] = chunk_of(
                coords, part, 3, nears, weights, hidden, gathered
            ).astype(BF)


def near_kernel(coords, down_own, down_other, hidden_ref, *refs):
    arrived, outs, gathered = refs[:4], refs[4:8], refs[8]
    hidden = [hidden_ref[n] for n in range(2)]
    weights = (down_own, down_other)
    for part in range(2):
        from_left, from_right = arrived[2 * part], arrived[2 * part + 1]
        left, right = outs[2 * part], outs[2 * part + 1]
        for r3, out, extra, half in ((1, left, from_right, 1), (2, right, from_left, 0)):
            for h in range(2):
                total = chunk_of(coords, part, r3, (2 * h, 2 * h + 1), weights, hidden, gathered)
                if h == half:
                    total = total + extra[...].astype(F32)
                out[16 * h : 16 * h + 16] = total.astype(BF)


def own_kernel(coords, down_own, down_other, hidden_ref, *refs):
    outs, gathered = refs[:2], refs[2]
    hidden = [hidden_ref[n] for n in range(2)]
    for part in range(2):
        for h in range(2):
            outs[part][16 * h : 16 * h + 16] = chunk_of(
                coords, part, 0, (2 * h, 2 * h + 1), (down_own, down_other), hidden, gathered
            ).astype(BF)


def down_call(kernel, coords, weights, extra, shapes):
    return pl.pallas_call(
        kernel,
        in_specs=[SMEM] + vmem(2 + len(extra)),
        out_specs=vmem(len(shapes)),
        out_shape=[jax.ShapeDtypeStruct(s, BF) for s in shapes],
        scratch_shapes=[pltpu.VMEM((256, weights[0].shape[1]), BF)],
        compiler_params=params(48),
    )(coords, *weights, *extra)


def finish_kernel(stream_ref, sums_ref, out_ref):
    total = stream_ref[...].astype(F32) + jnp.sum(sums_ref[...].astype(F32), axis=0)
    out_ref[...] = total.astype(BF)


def finish(stream, sums):
    return pl.pallas_call(
        finish_kernel,
        in_specs=vmem(2),
        out_specs=pl.BlockSpec(memory_space=pltpu.VMEM),
        out_shape=jax.ShapeDtypeStruct(stream.shape, BF),
        compiler_params=params(16),
    )(stream, sums)


def shift(a, axis, by):
    return lax.ppermute(a, axis, [(i, (i + by) % 4) for i in range(4)])


def direct_gather(a, axis):
    return a, shift(a, axis, 1), shift(a, axis, -1), shift(a, axis, 2)


def ring_gather(a, axis):
    half = a.shape[0] // 2
    left, right = shift(a, axis, 1), shift(a, axis, -1)
    return a, left, right, shift(left[:half], axis, 1), shift(right[half:], axis, -1)


def add(*terms):
    return sum(t.astype(F32) for t in terms).astype(BF)


def all_to_all(a, axis):
    return lax.all_to_all(a, axis, split_axis=0, concat_axis=0, tiled=True)


AXES = (("y", "x"), ("x", "y"))
SWAP = [(0, 1), (1, 0)]


def per_device(
    queries,
    fresh_token_key,
    fresh_token_value,
    key_value_pool,
    request_block_map,
    lengths,
    row_counts,
    move_src,
    move_dst,
    move_count,
    residual,
    out_proj,
    w_gate,
    w_up,
    w_down,
):
    x, y, z = lax.axis_index("x"), lax.axis_index("y"), lax.axis_index("z")
    core = lax.axis_index("core")
    rank = lax.axis_index(("y", "z"))
    group = lax.axis_index(("x", "core"))
    coords = jnp.stack([y, x, z]).astype(jnp.int32)
    ranks, _, cap = move_src.shape
    slots = queries.shape[0]

    source = lax.dynamic_index_in_dim(move_src, rank, 0, keepdims=False).reshape(-1)
    parcel = parcels(source, key_value_pool)
    parcel = parcel.reshape((ranks, cap) + key_value_pool.shape[1:])
    arrived = all_to_all(parcel, ("y", "z")).reshape((ranks * cap,) + key_value_pool.shape[1:])
    target = lax.dynamic_index_in_dim(move_dst, rank, 1, keepdims=False)
    count = lax.dynamic_index_in_dim(move_count, rank, 1, keepdims=False)
    target = jnp.where(jnp.arange(cap)[None, :] < count[:, None], target, -1).reshape(-1)
    depth = request_block_map.shape[1]
    start = jnp.arange(depth, dtype=jnp.int32) * TOKENS
    inside = jnp.clip(lengths[:, None] - start[None, :], 0, TOKENS).astype(jnp.int32)
    hit = request_block_map.reshape(1, -1) == target[:, None]
    slot_of = jnp.arange(request_block_map.size, dtype=jnp.int32) // depth
    taker = jnp.max(jnp.where(hit, slot_of[None, :], -1), axis=1)
    limit = jnp.max(jnp.where(hit, inside.reshape(1, -1), 0), axis=1)
    token = jnp.arange(TOKENS, dtype=jnp.int32)
    taker = jnp.where(token[None, :] < limit[:, None], taker[:, None], -1).reshape(1, -1)
    stays = jnp.where(jnp.any(hit, axis=0).reshape(inside.shape), 0, inside)
    allowed = (token[None, None, :] < stays[:, :, None]).astype(jnp.int32).reshape(slots, -1)

    n = np.arange(256)
    which, part, xs, j = n // 128, n // 64 % 2, n // 16 % 4, n % 16
    column = 64 * xs + 16 * part + j
    owner = jnp.where(which == 0, core, 1 - core)
    order = (jnp.arange(256)[None, :] == (column + 32 * owner)[:, None]).astype(BF)
    up_own, up_other, down_own, down_other = split_weights(order, w_gate, w_up, w_down)
    weights = (up_own, lax.ppermute(up_other, "core", SWAP))
    down_weights = (down_own, lax.ppermute(down_other, "core", SWAP))
    mine = lax.dynamic_slice_in_dim(residual, group * 32, 32, 1).T
    mine = jnp.pad(mine, ((0, 0), (0, out_proj.shape[0] - mine.shape[1])))
    columns = out_proj.T
    columns = jnp.concatenate([columns[:128], mine[:16], columns[128:], mine[16:]])
    columns, _ = lax.optimization_barrier((columns, parcel))
    out_weight = direct_gather(columns, "y")
    counts = lax.dynamic_slice_in_dim(row_counts, y * 8, 8, 0)
    live = (jnp.arange(slots)[None, :] < counts[:, None]).reshape(1, 8 * slots)

    table, up_own, down_own = lax.optimization_barrier((request_block_map, up_own, down_own))
    q = queries.reshape(slots * GROUP, HEAD).astype(F32)
    local = attend_pool(
        table, q, fresh_token_key.astype(F32), fresh_token_value.astype(F32), allowed,
        key_value_pool,
    )
    weights, down_weights = (up_own, weights[1]), (down_own, down_weights[1])
    attended = attend_moved(q, taker, arrived, *local)
    rows = all_to_all(attended, "z").reshape(8 * slots, attended.shape[2])
    partial, mine = project(coords, rows, out_weight)
    partial = all_to_all(partial, ("x", "core"))
    piece = mine.astype(F32) + jnp.sum(partial.astype(F32), axis=0)
    piece = jnp.where(live, piece, F32(0.0)).astype(BF)
    spread = all_to_all(jnp.broadcast_to(piece[None], (8,) + piece.shape), "z")
    spread = spread.reshape(32, 2, 16, 8 * slots)
    gathered = lax.optimization_barrier(
        [direct_gather(spread[:, part], near) for part, (near, _) in enumerate(AXES)]
    )
    gathered = [jnp.concatenate(g) for g in gathered]
    pieces = []
    for part, (_, far) in enumerate(AXES):
        pieces += ring_gather(gathered[part], far)
    gu_own, gu_other, stream = gate_up(coords, *weights, pieces)
    in_other = lax.ppermute(gu_own, "core", SWAP)
    in_own = lax.ppermute(gu_other, "core", SWAP)

    width = gu_own.shape[2]
    half, whole = (16, 16, width), (32, 16, width)
    *far_sums, hidden = down_call(
        far_kernel,
        coords,
        down_weights,
        (gu_own, gu_other, in_own, in_other),
        [half] * 4 + [(2, HEAD, width)],
    )
    arriving = []
    for part, (_, far) in enumerate(AXES):
        arriving += [shift(far_sums[2 * part], far, 1), shift(far_sums[2 * part + 1], far, -1)]
    own = down_call(own_kernel, coords, down_weights, (hidden,), [whole] * 2)
    sums = down_call(near_kernel, coords, down_weights, (hidden, *arriving), [whole] * 4)
    landed = lax.optimization_barrier(
        [
            (shift(sums[2 * part + 1], far, 1), shift(sums[2 * part], far, -1))
            for part, (_, far) in enumerate(AXES)
        ]
    )
    second = []
    for part, (near, _) in enumerate(AXES):
        here, left, right, opposite = (
            add(own[part][8 * r : 8 * r + 8], *(a[8 * r : 8 * r + 8] for a in landed[part]))
            for r in range(4)
        )
        second.append(
            (here, shift(right, near, 1), shift(left, near, -1), shift(opposite, near, 2))
        )
    halves = [add(*terms) for terms in lax.optimization_barrier(second)]
    sums = all_to_all(jnp.concatenate(halves, axis=1), "z")
    return finish(stream, sums).T


def solution(mesh):
    mesh = Mesh(mesh.devices.reshape(4, 8, 4, 2), ("y", "z", "x", "core"))
    dp, tp = ("y", "z"), ("x", "core")
    return jax.shard_map(
        per_device,
        mesh=mesh,
        in_specs=(
            P(dp, tp),
            P(dp, tp),
            P(dp, tp),
            P(dp, None, None, tp),
            P(dp, None),
            P(dp),
            P(),
            P(),
            P(),
            P(),
            P(None, dp),
            P(tp, dp),
            P(dp + tp, None),
            P(dp + tp, None),
            P(dp + tp, None),
        ),
        out_specs=P(None, dp + tp),
        check_vma=False,
    )
```

```python
import jax
import jax.numpy as jnp
import numpy as np
from jax import lax
from jax.experimental import pallas as pl
from jax.experimental.pallas import tpu as pltpu
from jax.sharding import Mesh, PartitionSpec as P

HEAD = 128
GROUP = 8
TOKENS = 16
BF = jnp.bfloat16
F32 = jnp.float32
SCALE = np.float32(1.0) / np.sqrt(np.float32(HEAD))
NT = (((1,), (1,)), ((), ()))
NN = (((1,), (0,)), ((), ()))
REL = (0, 3, 1, 2)


def params(mib):
    return pltpu.CompilerParams(vmem_limit_bytes=mib * 2**20)


def vmem(n):
    return [pl.BlockSpec(memory_space=pltpu.VMEM)] * n


SMEM = pl.BlockSpec(memory_space=pltpu.SMEM)
ANY = pl.BlockSpec(memory_space=pl.ANY)


def weights_kernel(order_ref, gate_ref, up_ref, down_ref, own_ref, other_ref, down_own, down_other):
    order = order_ref[...]
    for j in range(gate_ref.shape[1] // 256):
        cols = slice(256 * j, 256 * j + 256)
        half = slice(128 * j, 128 * j + 128)
        for n, ref in enumerate((gate_ref, up_ref)):
            moved = lax.dot_general(ref[:, cols], order, NT, preferred_element_type=F32).astype(BF)
            rows = slice(n * moved.shape[0], (n + 1) * moved.shape[0])
            own_ref[rows, half] = moved[:, :128]
            other_ref[rows, half] = moved[:, 128:]
        moved = lax.dot_general(order, down_ref[:, cols], NT, preferred_element_type=F32).astype(BF)
        rows = moved.shape[1]
        for ref, part in ((down_own, moved[:128]), (down_other, moved[128:])):
            ref[half, :rows] = part
            ref[half, rows:] = jnp.zeros((128, ref.shape[1] - rows), BF)


def split_weights(order, w_gate, w_up, w_down):
    rows, width = w_gate.shape
    step = 1024
    half = step // 2
    return pl.pallas_call(
        weights_kernel,
        grid=(width // step,),
        in_specs=[pl.BlockSpec((256, 256), lambda i: (0, 0))]
        + [pl.BlockSpec((rows, step), lambda i: (0, i))] * 3,
        out_specs=[pl.BlockSpec((2 * rows, half), lambda i: (0, i))] * 2
        + [pl.BlockSpec((half, HEAD), lambda i: (i, 0))] * 2,
        out_shape=[jax.ShapeDtypeStruct((2 * rows, width // 2), BF)] * 2
        + [jax.ShapeDtypeStruct((width // 2, HEAD), BF)] * 2,
        compiler_params=params(58),
    )(order, w_gate, w_up, w_down)


def load_pool(pool_ref, blocks, sems):
    parts = sems.shape[0]
    rows = blocks.shape[0] // parts
    loads = [
        pltpu.make_async_copy(
            pool_ref.at[pl.ds(n * rows, rows)], blocks.at[pl.ds(n * rows, rows)], sems.at[n]
        )
        for n in range(parts)
    ]
    for load in loads:
        load.start()
    for load in loads:
        load.wait()


def parcel_kernel(source, pool_ref, out_ref, blocks, sems):
    load_pool(pool_ref, blocks, sems)

    def pick(n, carry):
        out_ref[n] = blocks[source[n]]
        return carry

    lax.fori_loop(0, out_ref.shape[0], pick, 0, unroll=8)


def parcels(source, pool):
    return pl.pallas_call(
        parcel_kernel,
        in_specs=[SMEM, ANY],
        out_specs=pl.BlockSpec(memory_space=pltpu.VMEM),
        out_shape=jax.ShapeDtypeStruct(source.shape + pool.shape[1:], BF),
        scratch_shapes=[pltpu.VMEM(pool.shape, BF), pltpu.SemaphoreType.DMA((8,))],
        compiler_params=params(58),
    )(source, pool)


def pool_kernel(
    table, q_ref, key_ref, value_ref, allowed_ref, pool_ref,
    out_ref, top_ref, total_ref, keys, values, scores,
):
    slots, depth = table.shape

    def fetch(i, carry):
        for j in range(depth):
            block = table[i, j]
            keys[i, j * TOKENS : (j + 1) * TOKENS, :] = pool_ref[block, 0]
            values[i, j * TOKENS : (j + 1) * TOKENS, :] = pool_ref[block, 1]
        return carry

    lax.fori_loop(0, slots, fetch, 0)
    for i in range(slots):
        rows = slice(i * GROUP, (i + 1) * GROUP)
        q = q_ref[rows, :]
        s = lax.dot_general(q.astype(BF), keys[i], NT, preferred_element_type=F32) * SCALE
        scores[rows, :] = jnp.where(allowed_ref[i : i + 1, :] > 0, s, F32(-1e30))
        own = jnp.sum(q * key_ref[i : i + 1, :], axis=1, keepdims=True) * SCALE
        out_ref[rows, :] = jnp.broadcast_to(own, (GROUP, HEAD))
    s = scores[...]
    own = out_ref[:, :1]
    top = jnp.maximum(jnp.max(s, axis=1, keepdims=True), own)
    e = jnp.where(s > F32(-1e29), jnp.exp(s - top), F32(0.0))
    own_e = jnp.exp(own - top)
    total = jnp.sum(e, axis=1, keepdims=True) + own_e
    scores[...] = e
    top_ref[...] = jnp.broadcast_to(top, top_ref.shape)
    total_ref[...] = jnp.broadcast_to(total, total_ref.shape)
    out_ref[...] = jnp.broadcast_to(own_e.astype(BF).astype(F32), out_ref.shape)
    for i in range(slots):
        rows = slice(i * GROUP, (i + 1) * GROUP)
        o = lax.dot_general(scores[rows, :].astype(BF), values[i], NN, preferred_element_type=F32)
        out_ref[rows, :] = o + out_ref[rows, :] * value_ref[i : i + 1, :]


def attend_pool(table, queries, fresh_key, fresh_value, allowed, pool):
    slots, depth = table.shape
    span = depth * TOKENS
    return pl.pallas_call(
        pool_kernel,
        in_specs=[SMEM] + vmem(5),
        out_specs=vmem(3),
        out_shape=[jax.ShapeDtypeStruct(queries.shape, F32)] * 3,
        scratch_shapes=[
            pltpu.VMEM((slots, span, HEAD), BF),
            pltpu.VMEM((slots, span, HEAD), BF),
            pltpu.VMEM((slots * GROUP, span), F32),
        ],
        compiler_params=params(20),
    )(table, queries, fresh_key, fresh_value, allowed, pool)


def moved_kernel(q_ref, owner_ref, arrived_ref, part_ref, top_ref, total_ref, out_ref, result):
    blocks = arrived_ref.shape[0]
    keys = arrived_ref[:, 0].reshape(blocks * TOKENS, HEAD)
    values = arrived_ref[:, 1].reshape(blocks * TOKENS, HEAD)
    s = lax.dot_general(q_ref[...].astype(BF), keys, NT, preferred_element_type=F32) * SCALE
    slot = lax.broadcasted_iota(jnp.int32, s.shape, 0) >> 3
    mine = slot == owner_ref[...]
    before = top_ref[:, :1]
    top = jnp.maximum(before, jnp.max(jnp.where(mine, s, F32(-1e30)), axis=1, keepdims=True))
    e = jnp.where(mine, jnp.exp(s - top), F32(0.0))
    keep = jnp.exp(before - top)
    total = total_ref[:, :1] * keep + jnp.sum(e, axis=1, keepdims=True)
    o = lax.dot_general(e.astype(BF), values, NN, preferred_element_type=F32)
    result[...] = (part_ref[...] * keep + o) / total
    slots = out_ref.shape[1]
    for h in range(GROUP):
        head = result[pl.ds(h, slots, stride=GROUP), :].astype(BF)
        for n in range(out_ref.shape[0]):
            out_ref[n, :, h * HEAD : (h + 1) * HEAD] = head


def attend_moved(queries, owner, arrived, part, top, total):
    slots = queries.shape[0] // GROUP
    return pl.pallas_call(
        moved_kernel,
        in_specs=vmem(6),
        out_specs=pl.BlockSpec(memory_space=pltpu.VMEM),
        out_shape=jax.ShapeDtypeStruct((8, slots, GROUP * HEAD), BF),
        scratch_shapes=[pltpu.VMEM(queries.shape, F32)],
        compiler_params=params(24),
    )(queries, owner, arrived, part, top, total)


def project_kernel(coords, rows_ref, columns_ref, out_ref, mine_ref):
    rows = rows_ref[...]
    lanes = pl.ds(pl.multiple_of(coords[0] * 128, 128), 128)
    for y in range(4):
        for part in range(2):
            at = 144 * part
            cols = lax.dot_general(
                columns_ref[y, at : at + 128, :], rows, NT, preferred_element_type=F32
            ).astype(BF)
            for n in range(4):
                out_ref[4 * part + n, 32 * y : 32 * y + 32, :] = cols[32 * n : 32 * n + 32]
            mine_ref[32 * y + 16 * part : 32 * y + 16 * part + 16, :] = columns_ref[
                y, at + 128 : at + 144, lanes
            ]


def project(coords, rows, columns):
    count = rows.shape[0]
    return pl.pallas_call(
        project_kernel,
        in_specs=[SMEM] + vmem(2),
        out_specs=vmem(2),
        out_shape=[
            jax.ShapeDtypeStruct((8, 128, count), BF),
            jax.ShapeDtypeStruct((128, count), BF),
        ],
        compiler_params=params(32),
    )(coords, rows, columns)


def up_kernel(coords, own_hbm, other_hbm, *refs):
    pieces, out_own, out_other, out_mine, stream, weights, sems = refs[:10], *refs[10:]
    rows = own_hbm.shape[0]
    loads = [
        pltpu.make_async_copy(own_hbm, weights.at[pl.ds(0, rows)], sems.at[0]),
        pltpu.make_async_copy(other_hbm, weights.at[pl.ds(rows, rows)], sems.at[1]),
    ]
    for load in loads:
        load.start()
    for part in range(2):
        own, left, right, far0, far1 = pieces[5 * part : 5 * part + 5]
        inner, outer = (0, 1) if part == 0 else (1, 0)
        for r3 in range(4):
            far = lax.rem(coords[outer] + REL[r3], 4)
            for r2 in range(4):
                near = lax.rem(coords[inner] + REL[r2], 4)
                y, x = (near, far) if part == 0 else (far, near)
                start = x * 16
                lane = pl.ds(pl.multiple_of(y * 128, 128), 128)
                for n in range(32):
                    if r3 < 3:
                        chunk = (own, left, right)[r3][r2 * 32 + n]
                    else:
                        chunk = (far0, far1)[r2 // 2][r2 % 2 * 32 + n]
                    row = (n % 4 * 8 + n // 4) * 128 + part * 64
                    stream[pl.ds(pl.multiple_of(row + start, 16), 16), lane] = chunk
    for load, out, at in zip(loads, (out_own, out_other), (0, rows)):
        load.wait()
        out[...] = lax.dot_general(
            weights[at : at + rows, :], stream[...], NN, preferred_element_type=F32
        ).reshape(out.shape)
    for part in range(2):
        row = (coords[0] * 8 + coords[2]) * 128 + part * 64 + coords[1] * 16
        out_mine[16 * part : 16 * part + 16, :] = stream[pl.ds(pl.multiple_of(row, 16), 16), :]


def gate_up(coords, own, other, pieces):
    width = 512
    return pl.pallas_call(
        up_kernel,
        in_specs=[SMEM, ANY, ANY] + vmem(10),
        out_specs=vmem(3),
        out_shape=[jax.ShapeDtypeStruct((2, own.shape[0] // 2, width), F32)] * 2
        + [jax.ShapeDtypeStruct((32, width), BF)],
        scratch_shapes=[
            pltpu.VMEM((own.shape[1], width), BF),
            pltpu.VMEM((2 * own.shape[0], own.shape[1]), BF),
            pltpu.SemaphoreType.DMA((2,)),
        ],
        compiler_params=params(48),
    )(coords, own, other, *pieces)


def chunk_of(coords, part, r3, nears, weight_refs, hidden, gathered):
    inner, outer = (0, 1) if part == 0 else (1, 0)
    far = lax.rem(coords[outer] + REL[r3], 4)
    total = None
    for ref, h in zip(weight_refs, hidden):
        for k, r2 in enumerate(nears):
            near = lax.rem(coords[inner] + REL[r2], 4)
            y, x = (near, far) if part == 0 else (far, near)
            for z in range(8):
                row = (y * 8 + z) * 128 + part * 64 + x * 16
                at = (k * 8 + z) * 16
                gathered[at : at + 16, :] = ref[pl.ds(pl.multiple_of(row, 16), 16), :]
        lhs = gathered[: len(nears) * 128, :]
        term = lax.dot_general(lhs, h, NN, preferred_element_type=F32)
        total = term if total is None else total + term
    return total.reshape(len(nears) * 8, 16, total.shape[1])


def far_kernel(coords, down_own, down_other, gu_own, gu_other, in_own, in_other, *refs):
    outs, hidden_ref, gathered = refs[:4], refs[4], refs[5]
    for n, (mine, theirs) in enumerate(((gu_own, in_own), (gu_other, in_other))):
        gate = mine[0] + theirs[0]
        up = mine[1] + theirs[1]
        rows = gate.shape[0]
        hidden_ref[n, :rows, :] = (gate * jax.nn.sigmoid(gate) * up).astype(BF)
        hidden_ref[n, rows:, :] = jnp.zeros((hidden_ref.shape[1] - rows, gate.shape[1]), BF)
    hidden = [hidden_ref[n] for n in range(2)]
    weights = (down_own, down_other)
    for part in range(2):
        for half in range(2):
            nears = (2 * half, 2 * half + 1)
            outs[2 * part + half][...] = chunk_of(
                coords, part, 3, nears, weights, hidden, gathered
            ).astype(BF)


def near_kernel(coords, down_own, down_other, hidden_ref, *refs):
    arrived, outs, gathered = refs[:4], refs[4:8], refs[8]
    hidden = [hidden_ref[n] for n in range(2)]
    weights = (down_own, down_other)
    for part in range(2):
        from_left, from_right = arrived[2 * part], arrived[2 * part + 1]
        left, right = outs[2 * part], outs[2 * part + 1]
        for r3, out, extra, half in ((1, left, from_right, 1), (2, right, from_left, 0)):
            for h in range(2):
                total = chunk_of(coords, part, r3, (2 * h, 2 * h + 1), weights, hidden, gathered)
                if h == half:
                    total = total + extra[...].astype(F32)
                out[16 * h : 16 * h + 16] = total.astype(BF)


def own_kernel(coords, down_own, down_other, hidden_ref, *refs):
    outs, gathered = refs[:2], refs[2]
    hidden = [hidden_ref[n] for n in range(2)]
    for part in range(2):
        for h in range(2):
            outs[part][16 * h : 16 * h + 16] = chunk_of(
                coords, part, 0, (2 * h, 2 * h + 1), (down_own, down_other), hidden, gathered
            ).astype(BF)


def down_call(kernel, coords, weights, extra, shapes):
    return pl.pallas_call(
        kernel,
        in_specs=[SMEM] + vmem(2 + len(extra)),
        out_specs=vmem(len(shapes)),
        out_shape=[jax.ShapeDtypeStruct(s, BF) for s in shapes],
        scratch_shapes=[pltpu.VMEM((256, weights[0].shape[1]), BF)],
        compiler_params=params(48),
    )(coords, *weights, *extra)


def finish_kernel(stream_ref, sums_ref, out_ref):
    total = stream_ref[...].astype(F32) + jnp.sum(sums_ref[...].astype(F32), axis=0)
    out_ref[...] = total.astype(BF)


def finish(stream, sums):
    return pl.pallas_call(
        finish_kernel,
        in_specs=vmem(2),
        out_specs=pl.BlockSpec(memory_space=pltpu.VMEM),
        out_shape=jax.ShapeDtypeStruct(stream.shape, BF),
        compiler_params=params(16),
    )(stream, sums)


def shift(a, axis, by):
    return lax.ppermute(a, axis, [(i, (i + by) % 4) for i in range(4)])


def direct_gather(a, axis):
    return a, shift(a, axis, 1), shift(a, axis, -1), shift(a, axis, 2)


def ring_gather(a, axis):
    half = a.shape[0] // 2
    left, right = shift(a, axis, 1), shift(a, axis, -1)
    return a, left, right, shift(left[:half], axis, 1), shift(right[half:], axis, -1)


def add(*terms):
    return sum(t.astype(F32) for t in terms).astype(BF)


def all_to_all(a, axis):
    return lax.all_to_all(a, axis, split_axis=0, concat_axis=0, tiled=True)


AXES = (("y", "x"), ("x", "y"))
SWAP = [(0, 1), (1, 0)]


def per_device(
    queries,
    fresh_token_key,
    fresh_token_value,
    key_value_pool,
    request_block_map,
    lengths,
    row_counts,
    move_src,
    move_dst,
    move_count,
    residual,
    out_proj,
    w_gate,
    w_up,
    w_down,
):
    x, y, z = lax.axis_index("x"), lax.axis_index("y"), lax.axis_index("z")
    core = lax.axis_index("core")
    rank = lax.axis_index(("y", "z"))
    group = lax.axis_index(("x", "core"))
    coords = jnp.stack([y, x, z]).astype(jnp.int32)
    ranks, _, cap = move_src.shape
    slots = queries.shape[0]

    source = lax.dynamic_index_in_dim(move_src, rank, 0, keepdims=False).reshape(-1)
    parcel = parcels(source, key_value_pool)
    parcel = parcel.reshape((ranks, cap) + key_value_pool.shape[1:])
    arrived = all_to_all(parcel, ("y", "z")).reshape((ranks * cap,) + key_value_pool.shape[1:])
    target = lax.dynamic_index_in_dim(move_dst, rank, 1, keepdims=False)
    count = lax.dynamic_index_in_dim(move_count, rank, 1, keepdims=False)
    target = jnp.where(jnp.arange(cap)[None, :] < count[:, None], target, -1).reshape(-1)
    depth = request_block_map.shape[1]
    start = jnp.arange(depth, dtype=jnp.int32) * TOKENS
    inside = jnp.clip(lengths[:, None] - start[None, :], 0, TOKENS).astype(jnp.int32)
    hit = request_block_map.reshape(1, -1) == target[:, None]
    slot_of = jnp.arange(request_block_map.size, dtype=jnp.int32) // depth
    taker = jnp.max(jnp.where(hit, slot_of[None, :], -1), axis=1)
    limit = jnp.max(jnp.where(hit, inside.reshape(1, -1), 0), axis=1)
    token = jnp.arange(TOKENS, dtype=jnp.int32)
    taker = jnp.where(token[None, :] < limit[:, None], taker[:, None], -1).reshape(1, -1)
    stays = jnp.where(jnp.any(hit, axis=0).reshape(inside.shape), 0, inside)
    allowed = (token[None, None, :] < stays[:, :, None]).astype(jnp.int32).reshape(slots, -1)

    n = np.arange(256)
    which, part, xs, j = n // 128, n // 64 % 2, n // 16 % 4, n % 16
    column = 64 * xs + 16 * part + j
    owner = jnp.where(which == 0, core, 1 - core)
    order = (jnp.arange(256)[None, :] == (column + 32 * owner)[:, None]).astype(BF)
    up_own, up_other, down_own, down_other = split_weights(order, w_gate, w_up, w_down)
    weights = (up_own, lax.ppermute(up_other, "core", SWAP))
    down_weights = (down_own, lax.ppermute(down_other, "core", SWAP))
    mine = lax.dynamic_slice_in_dim(residual, group * 32, 32, 1).T
    mine = jnp.pad(mine, ((0, 0), (0, out_proj.shape[0] - mine.shape[1])))
    columns = out_proj.T
    columns = jnp.concatenate([columns[:128], mine[:16], columns[128:], mine[16:]])
    out_weight = lax.all_gather(columns, "y")
    counts = lax.dynamic_slice_in_dim(row_counts, y * 8, 8, 0)
    live = (jnp.arange(slots)[None, :] < counts[:, None]).reshape(1, 8 * slots)

    table, up_own, down_own = lax.optimization_barrier((request_block_map, up_own, down_own))
    q = queries.reshape(slots * GROUP, HEAD).astype(F32)
    local = attend_pool(
        table, q, fresh_token_key.astype(F32), fresh_token_value.astype(F32), allowed,
        key_value_pool,
    )
    q, up_other, down_other = lax.optimization_barrier((q, weights[1], down_weights[1]))
    weights, down_weights = (up_own, up_other), (down_own, down_other)
    attended = attend_moved(q, taker, arrived, *local)
    rows = all_to_all(attended, "z").reshape(8 * slots, attended.shape[2])
    partial, mine = project(coords, rows, out_weight)
    partial = all_to_all(partial, ("x", "core"))
    piece = mine.astype(F32) + jnp.sum(partial.astype(F32), axis=0)
    piece = jnp.where(live, piece, F32(0.0)).astype(BF)
    spread = all_to_all(jnp.broadcast_to(piece[None], (8,) + piece.shape), "z")
    spread = spread.reshape(32, 2, 16, 8 * slots)
    gathered = lax.optimization_barrier(
        [direct_gather(spread[:, part], near) for part, (near, _) in enumerate(AXES)]
    )
    gathered = [jnp.concatenate(g) for g in gathered]
    pieces = []
    for part, (_, far) in enumerate(AXES):
        pieces += ring_gather(gathered[part], far)
    gu_own, gu_other, stream = gate_up(coords, *weights, pieces)
    in_other = lax.ppermute(gu_own, "core", SWAP)
    in_own = lax.ppermute(gu_other, "core", SWAP)

    width = gu_own.shape[2]
    half, whole = (16, 16, width), (32, 16, width)
    *far_sums, hidden = down_call(
        far_kernel,
        coords,
        down_weights,
        (gu_own, gu_other, in_own, in_other),
        [half] * 4 + [(2, HEAD, width)],
    )
    arriving = []
    for part, (_, far) in enumerate(AXES):
        arriving += [shift(far_sums[2 * part], far, 1), shift(far_sums[2 * part + 1], far, -1)]
    own = down_call(own_kernel, coords, down_weights, (hidden,), [whole] * 2)
    sums = down_call(near_kernel, coords, down_weights, (hidden, *arriving), [whole] * 4)
    landed = lax.optimization_barrier(
        [
            (shift(sums[2 * part + 1], far, 1), shift(sums[2 * part], far, -1))
            for part, (_, far) in enumerate(AXES)
        ]
    )
    second = []
    for part, (near, _) in enumerate(AXES):
        here, left, right, opposite = (
            add(own[part][8 * r : 8 * r + 8], *(a[8 * r : 8 * r + 8] for a in landed[part]))
            for r in range(4)
        )
        second.append(
            (here, shift(right, near, 1), shift(left, near, -1), shift(opposite, near, 2))
        )
    halves = [add(*terms) for terms in lax.optimization_barrier(second)]
    sums = all_to_all(jnp.concatenate(halves, axis=1), "z")
    return finish(stream, sums).T


def solution(mesh):
    mesh = Mesh(mesh.devices.reshape(4, 8, 4, 2), ("y", "z", "x", "core"))
    dp, tp = ("y", "z"), ("x", "core")
    return jax.shard_map(
        per_device,
        mesh=mesh,
        in_specs=(
            P(dp, tp),
            P(dp, tp),
            P(dp, tp),
            P(dp, None, None, tp),
            P(dp, None),
            P(dp),
            P(),
            P(),
            P(),
            P(),
            P(None, dp),
            P(tp, dp),
            P(dp + tp, None),
            P(dp + tp, None),
            P(dp + tp, None),
        ),
        out_specs=P(None, dp + tp),
        check_vma=False,
    )
```

```python
import jax
import jax.numpy as jnp
import numpy as np
from jax import lax
from jax.experimental import pallas as pl
from jax.experimental.pallas import tpu as pltpu
from jax.sharding import Mesh, PartitionSpec as P

HEAD = 128
GROUP = 8
TOKENS = 16
BF = jnp.bfloat16
F32 = jnp.float32
SCALE = np.float32(1.0) / np.sqrt(np.float32(HEAD))
NT = (((1,), (1,)), ((), ()))
NN = (((1,), (0,)), ((), ()))
REL = (0, 3, 1, 2)


def params(mib):
    return pltpu.CompilerParams(vmem_limit_bytes=mib * 2**20)


def vmem(n):
    return [pl.BlockSpec(memory_space=pltpu.VMEM)] * n


SMEM = pl.BlockSpec(memory_space=pltpu.SMEM)
ANY = pl.BlockSpec(memory_space=pl.ANY)


def weights_kernel(order_ref, gate_ref, up_ref, down_ref, own_ref, other_ref, down_own, down_other):
    order = order_ref[...]
    for j in range(gate_ref.shape[1] // 256):
        cols = slice(256 * j, 256 * j + 256)
        half = slice(128 * j, 128 * j + 128)
        for n, ref in enumerate((gate_ref, up_ref)):
            moved = lax.dot_general(ref[:, cols], order, NT, preferred_element_type=F32).astype(BF)
            rows = slice(n * moved.shape[0], (n + 1) * moved.shape[0])
            own_ref[rows, half] = moved[:, :128]
            other_ref[rows, half] = moved[:, 128:]
        moved = lax.dot_general(order, down_ref[:, cols], NT, preferred_element_type=F32).astype(BF)
        rows = moved.shape[1]
        for ref, part in ((down_own, moved[:128]), (down_other, moved[128:])):
            ref[half, :rows] = part
            ref[half, rows:] = jnp.zeros((128, ref.shape[1] - rows), BF)


def split_weights(order, w_gate, w_up, w_down):
    rows, width = w_gate.shape
    step = 1024
    half = step // 2
    return pl.pallas_call(
        weights_kernel,
        grid=(width // step,),
        in_specs=[pl.BlockSpec((256, 256), lambda i: (0, 0))]
        + [pl.BlockSpec((rows, step), lambda i: (0, i))] * 3,
        out_specs=[pl.BlockSpec((2 * rows, half), lambda i: (0, i))] * 2
        + [pl.BlockSpec((half, HEAD), lambda i: (i, 0))] * 2,
        out_shape=[jax.ShapeDtypeStruct((2 * rows, width // 2), BF)] * 2
        + [jax.ShapeDtypeStruct((width // 2, HEAD), BF)] * 2,
        compiler_params=params(58),
    )(order, w_gate, w_up, w_down)


def load_pool(pool_ref, blocks, sems):
    parts = sems.shape[0]
    rows = blocks.shape[0] // parts
    loads = [
        pltpu.make_async_copy(
            pool_ref.at[pl.ds(n * rows, rows)], blocks.at[pl.ds(n * rows, rows)], sems.at[n]
        )
        for n in range(parts)
    ]
    for load in loads:
        load.start()
    for load in loads:
        load.wait()


def parcel_kernel(source, pool_ref, out_ref, blocks, sems):
    load_pool(pool_ref, blocks, sems)

    def pick(n, carry):
        out_ref[n] = blocks[source[n]]
        return carry

    lax.fori_loop(0, out_ref.shape[0], pick, 0, unroll=8)


def parcels(source, pool):
    return pl.pallas_call(
        parcel_kernel,
        in_specs=[SMEM, ANY],
        out_specs=pl.BlockSpec(memory_space=pltpu.VMEM),
        out_shape=jax.ShapeDtypeStruct(source.shape + pool.shape[1:], BF),
        scratch_shapes=[pltpu.VMEM(pool.shape, BF), pltpu.SemaphoreType.DMA((8,))],
        compiler_params=params(58),
    )(source, pool)


def pool_kernel(
    table, q_ref, key_ref, value_ref, allowed_ref, pool_ref,
    out_ref, top_ref, total_ref, keys, values, scores,
):
    slots, depth = table.shape

    def fetch(i, carry):
        for j in range(depth):
            block = table[i, j]
            keys[i, j * TOKENS : (j + 1) * TOKENS, :] = pool_ref[block, 0]
            values[i, j * TOKENS : (j + 1) * TOKENS, :] = pool_ref[block, 1]
        return carry

    lax.fori_loop(0, slots, fetch, 0)
    for i in range(slots):
        rows = slice(i * GROUP, (i + 1) * GROUP)
        q = q_ref[rows, :]
        s = lax.dot_general(q.astype(BF), keys[i], NT, preferred_element_type=F32) * SCALE
        scores[rows, :] = jnp.where(allowed_ref[i : i + 1, :] > 0, s, F32(-1e30))
        own = jnp.sum(q * key_ref[i : i + 1, :], axis=1, keepdims=True) * SCALE
        out_ref[rows, :] = jnp.broadcast_to(own, (GROUP, HEAD))
    s = scores[...]
    own = out_ref[:, :1]
    top = jnp.maximum(jnp.max(s, axis=1, keepdims=True), own)
    e = jnp.where(s > F32(-1e29), jnp.exp(s - top), F32(0.0))
    own_e = jnp.exp(own - top)
    total = jnp.sum(e, axis=1, keepdims=True) + own_e
    scores[...] = e
    top_ref[...] = jnp.broadcast_to(top, top_ref.shape)
    total_ref[...] = jnp.broadcast_to(total, total_ref.shape)
    out_ref[...] = jnp.broadcast_to(own_e.astype(BF).astype(F32), out_ref.shape)
    for i in range(slots):
        rows = slice(i * GROUP, (i + 1) * GROUP)
        o = lax.dot_general(scores[rows, :].astype(BF), values[i], NN, preferred_element_type=F32)
        out_ref[rows, :] = o + out_ref[rows, :] * value_ref[i : i + 1, :]


def attend_pool(table, queries, fresh_key, fresh_value, allowed, pool):
    slots, depth = table.shape
    span = depth * TOKENS
    return pl.pallas_call(
        pool_kernel,
        in_specs=[SMEM] + vmem(5),
        out_specs=vmem(3),
        out_shape=[jax.ShapeDtypeStruct(queries.shape, F32)] * 3,
        scratch_shapes=[
            pltpu.VMEM((slots, span, HEAD), BF),
            pltpu.VMEM((slots, span, HEAD), BF),
            pltpu.VMEM((slots * GROUP, span), F32),
        ],
        compiler_params=params(20),
    )(table, queries, fresh_key, fresh_value, allowed, pool)


def moved_kernel(q_ref, owner_ref, arrived_ref, part_ref, top_ref, total_ref, out_ref, result):
    blocks = arrived_ref.shape[0]
    keys = arrived_ref[:, 0].reshape(blocks * TOKENS, HEAD)
    values = arrived_ref[:, 1].reshape(blocks * TOKENS, HEAD)
    s = lax.dot_general(q_ref[...].astype(BF), keys, NT, preferred_element_type=F32) * SCALE
    slot = lax.broadcasted_iota(jnp.int32, s.shape, 0) >> 3
    mine = slot == owner_ref[...]
    before = top_ref[:, :1]
    top = jnp.maximum(before, jnp.max(jnp.where(mine, s, F32(-1e30)), axis=1, keepdims=True))
    e = jnp.where(mine, jnp.exp(s - top), F32(0.0))
    keep = jnp.exp(before - top)
    total = total_ref[:, :1] * keep + jnp.sum(e, axis=1, keepdims=True)
    o = lax.dot_general(e.astype(BF), values, NN, preferred_element_type=F32)
    result[...] = (part_ref[...] * keep + o) / total
    slots = out_ref.shape[1]
    for h in range(GROUP):
        head = result[pl.ds(h, slots, stride=GROUP), :].astype(BF)
        for n in range(out_ref.shape[0]):
            out_ref[n, :, h * HEAD : (h + 1) * HEAD] = head


def attend_moved(queries, owner, arrived, part, top, total):
    slots = queries.shape[0] // GROUP
    return pl.pallas_call(
        moved_kernel,
        in_specs=vmem(6),
        out_specs=pl.BlockSpec(memory_space=pltpu.VMEM),
        out_shape=jax.ShapeDtypeStruct((8, slots, GROUP * HEAD), BF),
        scratch_shapes=[pltpu.VMEM(queries.shape, F32)],
        compiler_params=params(24),
    )(queries, owner, arrived, part, top, total)


def project_kernel(coords, rows_ref, columns_ref, out_ref, mine_ref):
    rows = rows_ref[...]
    lanes = pl.ds(pl.multiple_of(coords[0] * 128, 128), 128)
    for y in range(4):
        for part in range(2):
            at = 144 * part
            cols = lax.dot_general(
                columns_ref[y, at : at + 128, :], rows, NT, preferred_element_type=F32
            ).astype(BF)
            for n in range(4):
                out_ref[4 * part + n, 32 * y : 32 * y + 32, :] = cols[32 * n : 32 * n + 32]
            mine_ref[32 * y + 16 * part : 32 * y + 16 * part + 16, :] = columns_ref[
                y, at + 128 : at + 144, lanes
            ]


def project(coords, rows, columns):
    count = rows.shape[0]
    return pl.pallas_call(
        project_kernel,
        in_specs=[SMEM] + vmem(2),
        out_specs=vmem(2),
        out_shape=[
            jax.ShapeDtypeStruct((8, 128, count), BF),
            jax.ShapeDtypeStruct((128, count), BF),
        ],
        compiler_params=params(32),
    )(coords, rows, columns)


def up_kernel(coords, own_hbm, other_hbm, *refs):
    pieces, out_own, out_other, out_mine, stream, own_ref, other_ref, sems = refs[:10], *refs[10:]
    loads = [
        pltpu.make_async_copy(own_hbm, own_ref, sems.at[0]),
        pltpu.make_async_copy(other_hbm, other_ref, sems.at[1]),
    ]
    for load in loads:
        load.start()
    for part in range(2):
        own, left, right, far0, far1 = pieces[5 * part : 5 * part + 5]
        inner, outer = (0, 1) if part == 0 else (1, 0)
        for r3 in range(4):
            far = lax.rem(coords[outer] + REL[r3], 4)
            for r2 in range(4):
                near = lax.rem(coords[inner] + REL[r2], 4)
                y, x = (near, far) if part == 0 else (far, near)
                start = x * 16
                lane = pl.ds(pl.multiple_of(y * 128, 128), 128)
                for n in range(32):
                    if r3 < 3:
                        chunk = (own, left, right)[r3][r2 * 32 + n]
                    else:
                        chunk = (far0, far1)[r2 // 2][r2 % 2 * 32 + n]
                    row = (n % 4 * 8 + n // 4) * 128 + part * 64
                    stream[pl.ds(pl.multiple_of(row + start, 16), 16), lane] = chunk
    s = stream[...]
    for load, ref, out in zip(loads, (own_ref, other_ref), (out_own, out_other)):
        load.wait()
        for n in range(2):
            rows = slice(n * out.shape[1], (n + 1) * out.shape[1])
            out[n] = lax.dot_general(ref[rows, :], s, NN, preferred_element_type=F32)
    for part in range(2):
        row = (coords[0] * 8 + coords[2]) * 128 + part * 64 + coords[1] * 16
        out_mine[16 * part : 16 * part + 16, :] = stream[pl.ds(pl.multiple_of(row, 16), 16), :]


def gate_up(coords, own, other, pieces):
    width = 512
    return pl.pallas_call(
        up_kernel,
        in_specs=[SMEM, ANY, ANY] + vmem(10),
        out_specs=vmem(3),
        out_shape=[jax.ShapeDtypeStruct((2, own.shape[0] // 2, width), F32)] * 2
        + [jax.ShapeDtypeStruct((32, width), BF)],
        scratch_shapes=[
            pltpu.VMEM((own.shape[1], width), BF),
            pltpu.VMEM(own.shape, BF),
            pltpu.VMEM(own.shape, BF),
            pltpu.SemaphoreType.DMA((2,)),
        ],
        compiler_params=params(48),
    )(coords, own, other, *pieces)


def chunk_of(coords, part, r3, nears, weight_refs, hidden, gathered):
    inner, outer = (0, 1) if part == 0 else (1, 0)
    far = lax.rem(coords[outer] + REL[r3], 4)
    total = None
    for ref, h in zip(weight_refs, hidden):
        for k, r2 in enumerate(nears):
            near = lax.rem(coords[inner] + REL[r2], 4)
            y, x = (near, far) if part == 0 else (far, near)
            for z in range(8):
                row = (y * 8 + z) * 128 + part * 64 + x * 16
                at = (k * 8 + z) * 16
                gathered[at : at + 16, :] = ref[pl.ds(pl.multiple_of(row, 16), 16), :]
        lhs = gathered[: len(nears) * 128, :]
        term = lax.dot_general(lhs, h, NN, preferred_element_type=F32)
        total = term if total is None else total + term
    return total.reshape(len(nears) * 8, 16, total.shape[1])


def far_kernel(coords, down_own, down_other, gu_own, gu_other, in_own, in_other, *refs):
    outs, hidden_ref, gathered = refs[:4], refs[4], refs[5]
    for n, (mine, theirs) in enumerate(((gu_own, in_own), (gu_other, in_other))):
        gate = mine[0] + theirs[0]
        up = mine[1] + theirs[1]
        rows = gate.shape[0]
        hidden_ref[n, :rows, :] = (gate * jax.nn.sigmoid(gate) * up).astype(BF)
        hidden_ref[n, rows:, :] = jnp.zeros((hidden_ref.shape[1] - rows, gate.shape[1]), BF)
    hidden = [hidden_ref[n] for n in range(2)]
    weights = (down_own, down_other)
    for part in range(2):
        for half in range(2):
            nears = (2 * half, 2 * half + 1)
            outs[2 * part + half][...] = chunk_of(
                coords, part, 3, nears, weights, hidden, gathered
            ).astype(BF)


def near_kernel(coords, down_own, down_other, hidden_ref, *refs):
    arrived, outs, gathered = refs[:4], refs[4:8], refs[8]
    hidden = [hidden_ref[n] for n in range(2)]
    weights = (down_own, down_other)
    for part in range(2):
        from_left, from_right = arrived[2 * part], arrived[2 * part + 1]
        left, right = outs[2 * part], outs[2 * part + 1]
        for r3, out, extra, half in ((1, left, from_right, 1), (2, right, from_left, 0)):
            for h in range(2):
                total = chunk_of(coords, part, r3, (2 * h, 2 * h + 1), weights, hidden, gathered)
                if h == half:
                    total = total + extra[...].astype(F32)
                out[16 * h : 16 * h + 16] = total.astype(BF)


def own_kernel(coords, down_own, down_other, hidden_ref, *refs):
    outs, gathered = refs[:2], refs[2]
    hidden = [hidden_ref[n] for n in range(2)]
    for part in range(2):
        for h in range(2):
            outs[part][16 * h : 16 * h + 16] = chunk_of(
                coords, part, 0, (2 * h, 2 * h + 1), (down_own, down_other), hidden, gathered
            ).astype(BF)


def down_call(kernel, coords, weights, extra, shapes):
    return pl.pallas_call(
        kernel,
        in_specs=[SMEM] + vmem(2 + len(extra)),
        out_specs=vmem(len(shapes)),
        out_shape=[jax.ShapeDtypeStruct(s, BF) for s in shapes],
        scratch_shapes=[pltpu.VMEM((256, weights[0].shape[1]), BF)],
        compiler_params=params(48),
    )(coords, *weights, *extra)


def finish_kernel(stream_ref, sums_ref, out_ref):
    total = stream_ref[...].astype(F32) + jnp.sum(sums_ref[...].astype(F32), axis=0)
    out_ref[...] = total.astype(BF)


def finish(stream, sums):
    return pl.pallas_call(
        finish_kernel,
        in_specs=vmem(2),
        out_specs=pl.BlockSpec(memory_space=pltpu.VMEM),
        out_shape=jax.ShapeDtypeStruct(stream.shape, BF),
        compiler_params=params(16),
    )(stream, sums)


def shift(a, axis, by):
    return lax.ppermute(a, axis, [(i, (i + by) % 4) for i in range(4)])


def direct_gather(a, axis):
    return a, shift(a, axis, 1), shift(a, axis, -1), shift(a, axis, 2)


def ring_gather(a, axis):
    half = a.shape[0] // 2
    left, right = shift(a, axis, 1), shift(a, axis, -1)
    return a, left, right, shift(left[:half], axis, 1), shift(right[half:], axis, -1)


def add(*terms):
    return sum(t.astype(F32) for t in terms).astype(BF)


def all_to_all(a, axis):
    return lax.all_to_all(a, axis, split_axis=0, concat_axis=0, tiled=True)


AXES = (("y", "x"), ("x", "y"))
SWAP = [(0, 1), (1, 0)]


def per_device(
    queries,
    fresh_token_key,
    fresh_token_value,
    key_value_pool,
    request_block_map,
    lengths,
    row_counts,
    move_src,
    move_dst,
    move_count,
    residual,
    out_proj,
    w_gate,
    w_up,
    w_down,
):
    x, y, z = lax.axis_index("x"), lax.axis_index("y"), lax.axis_index("z")
    core = lax.axis_index("core")
    rank = lax.axis_index(("y", "z"))
    group = lax.axis_index(("x", "core"))
    coords = jnp.stack([y, x, z]).astype(jnp.int32)
    ranks, _, cap = move_src.shape
    slots = queries.shape[0]

    source = lax.dynamic_index_in_dim(move_src, rank, 0, keepdims=False).reshape(-1)
    parcel = parcels(source, key_value_pool)
    parcel = parcel.reshape((ranks, cap) + key_value_pool.shape[1:])
    arrived = all_to_all(parcel, ("y", "z")).reshape((ranks * cap,) + key_value_pool.shape[1:])
    target = lax.dynamic_index_in_dim(move_dst, rank, 1, keepdims=False)
    count = lax.dynamic_index_in_dim(move_count, rank, 1, keepdims=False)
    target = jnp.where(jnp.arange(cap)[None, :] < count[:, None], target, -1).reshape(-1)
    depth = request_block_map.shape[1]
    start = jnp.arange(depth, dtype=jnp.int32) * TOKENS
    inside = jnp.clip(lengths[:, None] - start[None, :], 0, TOKENS).astype(jnp.int32)
    hit = request_block_map.reshape(1, -1) == target[:, None]
    slot_of = jnp.arange(request_block_map.size, dtype=jnp.int32) // depth
    taker = jnp.max(jnp.where(hit, slot_of[None, :], -1), axis=1)
    limit = jnp.max(jnp.where(hit, inside.reshape(1, -1), 0), axis=1)
    token = jnp.arange(TOKENS, dtype=jnp.int32)
    taker = jnp.where(token[None, :] < limit[:, None], taker[:, None], -1).reshape(1, -1)
    stays = jnp.where(jnp.any(hit, axis=0).reshape(inside.shape), 0, inside)
    allowed = (token[None, None, :] < stays[:, :, None]).astype(jnp.int32).reshape(slots, -1)

    n = np.arange(256)
    which, part, xs, j = n // 128, n // 64 % 2, n // 16 % 4, n % 16
    column = 64 * xs + 16 * part + j
    owner = jnp.where(which == 0, core, 1 - core)
    order = (jnp.arange(256)[None, :] == (column + 32 * owner)[:, None]).astype(BF)
    up_own, up_other, down_own, down_other = split_weights(order, w_gate, w_up, w_down)
    weights = (up_own, lax.ppermute(up_other, "core", SWAP))
    down_weights = (down_own, lax.ppermute(down_other, "core", SWAP))
    mine = lax.dynamic_slice_in_dim(residual, group * 32, 32, 1).T
    mine = jnp.pad(mine, ((0, 0), (0, out_proj.shape[0] - mine.shape[1])))
    columns = out_proj.T
    columns = jnp.concatenate([columns[:128], mine[:16], columns[128:], mine[16:]])
    out_weight = lax.all_gather(columns, "y")
    counts = lax.dynamic_slice_in_dim(row_counts, y * 8, 8, 0)
    live = (jnp.arange(slots)[None, :] < counts[:, None]).reshape(1, 8 * slots)

    table, up_own, down_own = lax.optimization_barrier((request_block_map, up_own, down_own))
    q = queries.reshape(slots * GROUP, HEAD).astype(F32)
    local = attend_pool(
        table, q, fresh_token_key.astype(F32), fresh_token_value.astype(F32), allowed,
        key_value_pool,
    )
    q, up_other, down_other = lax.optimization_barrier((q, weights[1], down_weights[1]))
    weights, down_weights = (up_own, up_other), (down_own, down_other)
    attended = attend_moved(q, taker, arrived, *local)
    rows = all_to_all(attended, "z").reshape(8 * slots, attended.shape[2])
    partial, mine = project(coords, rows, out_weight)
    partial = all_to_all(partial, ("x", "core"))
    piece = mine.astype(F32) + jnp.sum(partial.astype(F32), axis=0)
    piece = jnp.where(live, piece, F32(0.0)).astype(BF)
    spread = all_to_all(jnp.broadcast_to(piece[None], (8,) + piece.shape), "z")
    spread = spread.reshape(32, 2, 16, 8 * slots)
    gathered = lax.optimization_barrier(
        [direct_gather(spread[:, part], near) for part, (near, _) in enumerate(AXES)]
    )
    gathered = [jnp.concatenate(g) for g in gathered]
    pieces = []
    for part, (_, far) in enumerate(AXES):
        pieces += ring_gather(gathered[part], far)
    gu_own, gu_other, stream = gate_up(coords, *weights, pieces)
    in_other = lax.ppermute(gu_own, "core", SWAP)
    in_own = lax.ppermute(gu_other, "core", SWAP)

    width = gu_own.shape[2]
    half, whole = (16, 16, width), (32, 16, width)
    *far_sums, hidden = down_call(
        far_kernel,
        coords,
        down_weights,
        (gu_own, gu_other, in_own, in_other),
        [half] * 4 + [(2, HEAD, width)],
    )
    arriving = []
    for part, (_, far) in enumerate(AXES):
        arriving += [shift(far_sums[2 * part], far, 1), shift(far_sums[2 * part + 1], far, -1)]
    own = down_call(own_kernel, coords, down_weights, (hidden,), [whole] * 2)
    sums = down_call(near_kernel, coords, down_weights, (hidden, *arriving), [whole] * 4)
    landed = lax.optimization_barrier(
        [
            (shift(sums[2 * part + 1], far, 1), shift(sums[2 * part], far, -1))
            for part, (_, far) in enumerate(AXES)
        ]
    )
    second = []
    for part, (near, _) in enumerate(AXES):
        here, left, right, opposite = (
            add(own[part][8 * r : 8 * r + 8], *(a[8 * r : 8 * r + 8] for a in landed[part]))
            for r in range(4)
        )
        second.append(
            (here, shift(right, near, 1), shift(left, near, -1), shift(opposite, near, 2))
        )
    halves = [add(*terms) for terms in lax.optimization_barrier(second)]
    sums = all_to_all(jnp.concatenate(halves, axis=1), "z")
    return finish(stream, sums).T


def solution(mesh):
    mesh = Mesh(mesh.devices.reshape(4, 8, 4, 2), ("y", "z", "x", "core"))
    dp, tp = ("y", "z"), ("x", "core")
    return jax.shard_map(
        per_device,
        mesh=mesh,
        in_specs=(
            P(dp, tp),
            P(dp, tp),
            P(dp, tp),
            P(dp, None, None, tp),
            P(dp, None),
            P(dp),
            P(),
            P(),
            P(),
            P(),
            P(None, dp),
            P(tp, dp),
            P(dp + tp, None),
            P(dp + tp, None),
            P(dp + tp, None),
        ),
        out_specs=P(None, dp + tp),
        check_vma=False,
    )
```
